32 devices in a mesh: dp: 16 (over z, x, core), mp: 2 (over y).
Axes of the slice: x: 2, y: 2, z: 4, core: 2. Of those that a mesh axis runs over, the one named last changes fastest.
Arguments:
- tokens: bfloat16 [6400, 1792], P('dp', 'mp'), may hold values from -6 to 6
- cotangent: bfloat16 [6400, 1792], P('dp', 'mp'), may hold values from -6 to 6
- master: float32 [1792, 4, 1792], P('dp', None, 'mp')
- moment_one: float32 [1792, 4, 1792], P('dp', None, 'mp'), may hold values from -4 to 4
- moment_two: float32 [1792, 4, 1792], P('dp', None, 'mp'), may hold values from 0.01 to 1
- ln_gain: float32 [1792], replicated, may hold values from 0.1 to 1.9
- ln_bias: float32 [1792], replicated, may hold values from -3 to 3
- norm_moment_one: float32 [2, 1792], replicated, may hold values from -4 to 4
- norm_moment_two: float32 [2, 1792], replicated, may hold values from 0.01 to 1
- image_count: int32 [16], P('dp'), may hold values from 1 to 25, as said below
- tokens_per_image: int32 [16], P('dp'), may hold values from 16 to 400, as said below
Outputs:
- block_out: bfloat16 [6400, 1792], P('dp', 'mp')
- input_grad: bfloat16 [6400, 1792], P('dp', 'mp')
- new_master: float32 [1792, 4, 1792], P('dp', None, 'mp')
- new_moment_one: float32 [1792, 4, 1792], P('dp', None, 'mp')
- new_moment_two: float32 [1792, 4, 1792], P('dp', None, 'mp')
- new_gain: float32 [1792], replicated
- new_bias: float32 [1792], replicated
- new_norm_moment_one: float32 [2, 1792], replicated
- new_norm_moment_two: float32 [2, 1792], replicated
The draws below stay inside these ranges and needn't reach their ends.
Inputs may be any that keep to these rules, and one draw needn't show every extreme that they name: `tokens_per_image`: A square number s * s; some group has exactly 400. image_count[g] * tokens_per_image[g] is at most 400 for every group g.
All inputs are finite; a program needn't handle non-finite values.
Results may differ from the reference program's by a relative error of at most 0.0085.
Values may be sent and summed in bfloat16 or wider, within the bound.
No kernel may reach another device: no remote copies, remote signals or barrier semaphores. Data moves between devices by JAX's collectives and lax.ppermute only.
A program may use at most 192 MiB of HBM per device.

```python
import math
import jax
import jax.numpy as jnp
from jax import lax

D = 1792
HEADS = 16
HEAD_DIM = 112
GRID = 20
TOK_DEV = 400
GROUPS = 16
TOKENS = 6400
HD = 1792
N_DP = 16
N_MP = 2


def group_plan(key):
    folded = jax.random.fold_in(key, 11)
    side_key, pick_key, count_key = jax.random.split(folded, 3)
    lowest = max(2, GRID // 5)
    side_cells = jax.random.randint(side_key, (GROUPS,), lowest, GRID + 1)
    chosen = jax.random.randint(pick_key, (), 0, GROUPS)
    coarse = (chosen + 1) % GROUPS
    places = jnp.arange(GROUPS)
    side_cells = jnp.where(places == chosen, GRID, side_cells)
    side_cells = jnp.where(places == coarse, lowest, side_cells)
    lengths = side_cells * side_cells
    most_images = GRID * GRID // lengths
    least_images = jnp.maximum(1, most_images // 2)
    counts = jax.random.randint(count_key, (GROUPS,), least_images, most_images + 1)
    counts = jnp.where(places == coarse, most_images, counts)
    return (counts.astype(jnp.int32), lengths.astype(jnp.int32))


def draw_image_count(key, part):
    return group_plan(key)[0]


def draw_tokens_per_image(key, part):
    return group_plan(key)[1]


def draw_master(key, part):
    width_all = HEADS * HEAD_DIM
    first_key = jax.random.fold_in(jax.random.fold_in(key, 23), 0)
    drawn_all = jax.random.normal(first_key, (D, 4, width_all), jnp.float32) * D ** (-0.5)
    return drawn_all


def shard_levels(key, dims, shards, low, high):
    level, own = 1.0, jax.random.fold_in(key, 6)
    for axis_at, shards_of in shards:
        heights = jnp.exp(jax.random.uniform(jax.random.fold_in(own, axis_at), (shards_of,), jnp.float32, low / len(shards), high / len(shards)))
        level = level * jnp.repeat(heights, dims[axis_at] // shards_of).reshape([-1 if axis == axis_at else 1 for axis in range(len(dims))])
    return level


def scatter_about(key, shape, scale, bound, shards=(), kind=jnp.bfloat16):
    entries = scale * jax.random.normal(key, shape, jnp.float32)
    if shards:
        entries = entries * shard_levels(key, shape, shards, -0.22, 0.18)
    return jnp.clip(entries, -bound, bound).astype(kind)


def setup_inputs(seed: int = 0) -> dict:
    splits = jax.random.split(jax.random.key(seed), 12)
    return {
        "tokens": scatter_about(splits[0], (TOKENS, D), 1.0, 6.0, ((0, 16), (1, 2))),
        "cotangent": scatter_about(splits[1], (TOKENS, D), 1.0, 6.0, ((0, 16), (1, 2))),
        "master": draw_master(jax.random.fold_in(splits[11], 71), 0),
        "moment_one": scatter_about(splits[3], (D, 4, HD), 0.5, 4.0, ((0, 16), (2, 2)), jnp.float32),
        "moment_two": jnp.clip(jnp.exp(math.log(1.0) - 4.6051702 * jax.random.uniform(splits[4], (D, 4, HD), jnp.float32) ** shard_levels(splits[4], (D, 4, HD), ((0, 16), (2, 2)), -0.2, 0.2)), 0.01, 1.0),
        "ln_gain": jnp.clip(1.0 + 0.18 * jax.random.normal(splits[5], (D,), jnp.float32), 0.1, 1.9),
        "ln_bias": scatter_about(splits[6], (D,), 0.5, 3.0, (), jnp.float32),
        "norm_moment_one": scatter_about(splits[7], (2, D), 0.5, 4.0, (), jnp.float32),
        "norm_moment_two": jnp.clip(jnp.exp(jax.random.uniform(splits[8], (2, D), jnp.float32, math.log(0.01), math.log(1.0))), 0.01, 1.0),
        "image_count": draw_image_count(jax.random.fold_in(splits[11], 71), 0),
        "tokens_per_image": draw_tokens_per_image(jax.random.fold_in(splits[11], 71), 0),
    }


eps_norm = 1e-06
beta_one = 0.9
beta_two = 0.95
learn_rate = 0.01
decay_rate = 0.1
adam_eps = 1e-08
step_count = 10.0

def layer_norm(row_block, gain, shift):
    values = row_block.astype(jnp.float32)
    center = lax.optimization_barrier(jnp.mean(values, axis=-1, keepdims=True))
    shifted = values - center
    spread = lax.optimization_barrier(jnp.mean(shifted * shifted, axis=-1, keepdims=True))
    inverse = lax.rsqrt(spread + eps_norm)
    normed = shifted * inverse
    return (normed, inverse, (normed * gain + shift).astype(jnp.bfloat16))

def same_image(image_here, length_here, total_rows):
    places = jnp.arange(total_rows, dtype=jnp.int32)
    live_rows = places < image_here * length_here
    labels = jnp.where(live_rows, places // length_here, jnp.int32(-1))
    return (live_rows, labels[:, None] == labels[None, :])

def half_block(normed_low, weights, allowed, grad_full):
    wide = jnp.float32
    row_count = normed_low.shape[0]
    heads_here = weights.shape[2] // HEAD_DIM
    score_scale = HEAD_DIM ** (-0.5)
    projected = jnp.einsum('td,dkh->kth', normed_low.astype(wide), weights[:, :3].astype(wide)).astype(jnp.bfloat16)
    query_rows = projected[0].reshape(row_count, heads_here, HEAD_DIM)
    key_rows = projected[1].reshape(row_count, heads_here, HEAD_DIM)
    value_rows = projected[2].reshape(row_count, heads_here, HEAD_DIM)
    scores = jnp.einsum('qhd,khd->hqk', query_rows.astype(wide), key_rows.astype(wide)) * score_scale
    scores = jnp.where(allowed[None], scores, -1e+30)
    row_max = lax.optimization_barrier(jnp.max(scores, axis=-1, keepdims=True))
    raised = jnp.exp(scores - row_max)
    prob_full = raised / lax.optimization_barrier(jnp.sum(raised, axis=-1, keepdims=True))
    prob_half = prob_full.astype(jnp.bfloat16)
    mixed = jnp.einsum('hqk,khd->qhd', prob_half.astype(wide), value_rows.astype(wide)).astype(jnp.bfloat16)
    mixed = mixed.reshape(row_count, heads_here * HEAD_DIM)
    out_weight = weights[:, 3]
    out_part = jnp.einsum('th,dh->td', mixed.astype(wide), out_weight.astype(wide))
    out_grad = jnp.einsum('td,th->dh', grad_full.astype(wide), mixed.astype(wide))
    mixed_grad = jnp.dot(grad_full, out_weight, preferred_element_type=jnp.float32).astype(jnp.bfloat16)
    mixed_grad = mixed_grad.reshape(row_count, heads_here, HEAD_DIM)
    prob_grad = jnp.einsum('qhd,khd->hqk', mixed_grad.astype(wide), value_rows.astype(wide))
    value_grad = jnp.einsum('hqk,qhd->khd', prob_half.astype(wide), mixed_grad.astype(wide)).astype(jnp.bfloat16)
    delta = lax.optimization_barrier(jnp.sum(prob_full * prob_grad, axis=-1, keepdims=True))
    score_grad = (prob_full * (prob_grad - delta) * score_scale).astype(jnp.bfloat16)
    query_grad = jnp.einsum('hqk,khd->qhd', score_grad.astype(wide), key_rows.astype(wide)).astype(jnp.bfloat16)
    key_grad = jnp.einsum('hqk,qhd->khd', score_grad.astype(wide), query_rows.astype(wide)).astype(jnp.bfloat16)
    proj_grad = jnp.stack([query_grad, key_grad, value_grad]).reshape(3, row_count, heads_here * HEAD_DIM)
    norm_grad = jnp.einsum('kth,dkh->td', proj_grad.astype(wide), weights[:, :3].astype(wide))
    inner_grad = jnp.einsum('td,kth->dkh', normed_low.astype(wide), proj_grad.astype(wide))
    grads = jnp.concatenate([inner_grad, out_grad[:, None]], axis=1)
    return (out_part, norm_grad, grads)

def adam_update(weight_now, moment_first, moment_second, gradient, decay):
    first_new = beta_one * moment_first + (1.0 - beta_one) * gradient
    second_new = beta_two * moment_second + (1.0 - beta_two) * gradient * gradient
    first_hat = first_new / (1.0 - beta_one ** step_count)
    second_hat = second_new / (1.0 - beta_two ** step_count)
    weight_new = weight_now - learn_rate * (first_hat / (jnp.sqrt(second_hat) + adam_eps) + decay * weight_now)
    return (weight_new, first_new, second_new)

def reference(tokens, cotangent, master, moment_one, moment_two, ln_gain, ln_bias, norm_moment_one, norm_moment_two, image_count, tokens_per_image):
    weights = master.astype(jnp.bfloat16)
    width_here = HEADS * HEAD_DIM // N_MP
    token_blocks = tokens.reshape(N_DP, TOK_DEV, D)
    cot_blocks = cotangent.reshape(N_DP, TOK_DEV, D)

    def one_group(carry, inputs):
        grad_total, gain_total, bias_total = carry
        block_rows, cot_rows, image_here, length_here = inputs
        normed, inverse, normed_low = layer_norm(block_rows, ln_gain, ln_bias)
        live_rows, allowed = same_image(image_here, length_here, TOK_DEV)
        grad_full = jnp.where(live_rows[:, None], cot_rows, jnp.zeros_like(cot_rows))
        out_sum = jnp.zeros((TOK_DEV, D), jnp.float32)
        input_sum = jnp.zeros((TOK_DEV, D), jnp.float32)
        pieces = []
        for shard_index in range(N_MP):
            part_weights = weights[:, :, shard_index * width_here:(shard_index + 1) * width_here]
            out_part, norm_grad, grads = half_block(normed_low, part_weights, allowed, grad_full)
            out_sum = out_sum + lax.optimization_barrier(out_part.astype(jnp.bfloat16)).astype(jnp.float32)
            gain_total = gain_total + lax.optimization_barrier(jnp.sum(norm_grad * normed, axis=0))
            bias_total = bias_total + lax.optimization_barrier(jnp.sum(norm_grad, axis=0))
            scaled = norm_grad * ln_gain
            input_part = inverse * (scaled - lax.optimization_barrier(jnp.mean(scaled, axis=-1, keepdims=True)) - normed * lax.optimization_barrier(jnp.mean(scaled * normed, axis=-1, keepdims=True)))
            input_sum = input_sum + lax.optimization_barrier(input_part.astype(jnp.bfloat16)).astype(jnp.float32)
            pieces.append(grads)
        grad_total = grad_total + jnp.concatenate(pieces, axis=2)
        block_out = (block_rows.astype(jnp.float32) + out_sum).astype(jnp.bfloat16)
        input_grad = (grad_full.astype(jnp.float32) + input_sum).astype(jnp.bfloat16)
        return ((grad_total, gain_total, bias_total), (block_out, input_grad))
    start_carry = (jnp.zeros((D, 4, HEADS * HEAD_DIM), jnp.float32), jnp.zeros((D,), jnp.float32), jnp.zeros((D,), jnp.float32))
    totals, outputs = lax.scan(one_group, start_carry, (token_blocks, cot_blocks, image_count, tokens_per_image))
    grad_total, gain_total, bias_total = totals
    block_out = outputs[0].reshape(N_DP * TOK_DEV, D)
    input_grad = outputs[1].reshape(N_DP * TOK_DEV, D)
    weight_grad = grad_total / N_DP
    new_master, new_moment_one, new_moment_two = adam_update(master, moment_one, moment_two, weight_grad, decay_rate)
    norm_param_grad = jnp.stack([gain_total, bias_total]) / N_DP
    stacked_params = jnp.stack([ln_gain, ln_bias])
    new_norm, new_norm_moment_one, new_norm_moment_two = adam_update(stacked_params, norm_moment_one, norm_moment_two, norm_param_grad, 0.0)
    return (block_out, input_grad, new_master, new_moment_one, new_moment_two, new_norm[0], new_norm[1], new_norm_moment_one, new_norm_moment_two)
```

```python
import functools

import jax
import jax.numpy as jnp
from jax import lax
from jax.experimental import pallas as pl
from jax.experimental.pallas import tpu as pltpu
from jax.sharding import PartitionSpec as P

HEAD_DIM = 112
LANES = 128

eps_norm = 1e-06
beta_one = 0.9
beta_two = 0.95
learn_rate = 0.01
decay_rate = 0.1
adam_eps = 1e-08
step_count = 10.0

bf16 = jnp.bfloat16
f32 = jnp.float32
WHOLE = pl.BlockSpec(memory_space=pltpu.VMEM)
SCALARS = pl.BlockSpec(memory_space=pltpu.SMEM)
ANYWHERE = pl.BlockSpec(memory_space=pl.ANY)
BIG = pltpu.CompilerParams(vmem_limit_bytes=56 * 1024 * 1024)


def round_up(value, unit):
    return -(-value // unit) * unit


def nt_dot(left, right):
    return lax.dot_general(left, right, (((1,), (1,)), ((), ())), preferred_element_type=f32)


def nn_dot(left, right):
    return jnp.dot(left, right, preferred_element_type=f32)


def layer_norm(row_block, gain, shift):
    values = row_block.astype(f32)
    center = jnp.mean(values, axis=-1, keepdims=True)
    shifted = values - center
    spread = jnp.mean(shifted * shifted, axis=-1, keepdims=True)
    inverse = lax.rsqrt(spread + eps_norm)
    normed = shifted * inverse
    return (normed, inverse, (normed * gain + shift).astype(bf16))


def adam_update(weight_now, moment_first, moment_second, gradient, decay):
    first_new = beta_one * moment_first + (1.0 - beta_one) * gradient
    second_new = beta_two * moment_second + (1.0 - beta_two) * gradient * gradient
    first_hat = first_new / (1.0 - beta_one**step_count)
    second_hat = second_new / (1.0 - beta_two**step_count)
    weight_new = weight_now - learn_rate * (
        first_hat / (jnp.sqrt(second_hat) + adam_eps) + decay * weight_now
    )
    return (weight_new, first_new, second_new)


class Plan:
    def __init__(self, columns):
        self.kind = columns // 2
        self.both = 2 * self.kind
        self.start = self.kind // LANES * LANES
        self.base = self.kind - self.start
        self.wide = self.both - self.start
        self.heads = self.kind // HEAD_DIM

    def window(self, head, base):
        low = base + head * HEAD_DIM
        high = low + HEAD_DIM
        return (low // LANES * LANES, min(self.wide, round_up(high, LANES)), low, high)


def pack_kernel(plan, master_ref, *outs):
    for chunk in range(2):
        for pair, kinds in enumerate(((0, 3), (1, 2))):
            columns = [
                master_ref[:, kind, chunk * plan.kind : (chunk + 1) * plan.kind] for kind in kinds
            ]
            outs[2 * chunk + pair][...] = jnp.concatenate(columns, axis=1).astype(bf16)


def pack(plan, master):
    out = jax.ShapeDtypeStruct((master.shape[0], plan.both), bf16)
    return pl.pallas_call(
        functools.partial(pack_kernel, plan),
        out_shape=[out] * 4,
        in_specs=[WHOLE],
        out_specs=[WHOLE] * 4,
        compiler_params=BIG,
        name="pack",
    )(master)


def project_kernel(plan, count, place_ref, normed_ref, grad_ref, *rest):
    blocks, rest = rest[: 2 * count], rest[2 * count :]
    query_ref, key_ref, value_ref, mixed_grad_ref, full_qo, full_kv, held_qo, held_kv, sems, outs = rest
    held = (held_qo, held_kv)
    rows = blocks[0].shape[0]
    copies = []
    for pair in range(2):
        for at in range(count):
            first = place_ref[at] * rows
            if rows % 16 == 0:
                first = pl.multiple_of(first, 16)
            copy = pltpu.make_async_copy(
                blocks[pair * count + at], held[pair].at[pl.ds(first, rows)], sems.at[pair * count + at]
            )
            copy.start()
            copies.append(copy)
    left, right = slice(0, plan.wide), slice(plan.start, plan.both)
    live = lax.broadcasted_iota(jnp.int32, (1, plan.wide), 1) >= plan.base
    for copy in copies[:count]:
        copy.wait()
    keep_qo = pltpu.make_async_copy(held_qo, full_qo, outs.at[0])
    keep_qo.start()
    query_ref[...] = nn_dot(normed_ref[...], held_qo[:, left]).astype(bf16)
    mixed_grad = nn_dot(grad_ref[...], held_qo[:, right])
    mixed_grad_ref[...] = jnp.where(live, mixed_grad, 0.0).astype(bf16)
    for copy in copies[count:]:
        copy.wait()
    keep_kv = pltpu.make_async_copy(held_kv, full_kv, outs.at[1])
    keep_kv.start()
    key_ref[...] = nn_dot(normed_ref[...], held_kv[:, left]).astype(bf16)
    value_ref[...] = nn_dot(normed_ref[...], held_kv[:, right]).astype(bf16)
    keep_qo.wait()
    keep_kv.wait()


def project(plan, places, normed_low, grad_rows, blocks):
    count = len(blocks) // 2
    rows, depth = normed_low.shape
    out = jax.ShapeDtypeStruct((rows, plan.wide), bf16)
    full = jax.ShapeDtypeStruct((depth, plan.both), bf16)
    return pl.pallas_call(
        functools.partial(project_kernel, plan, count),
        out_shape=[out] * 4 + [full] * 2,
        in_specs=[SCALARS, WHOLE, WHOLE] + [ANYWHERE] * (2 * count),
        out_specs=[WHOLE] * 4 + [ANYWHERE] * 2,
        scratch_shapes=[
            pltpu.VMEM((depth, plan.both), bf16),
            pltpu.VMEM((depth, plan.both), bf16),
            pltpu.SemaphoreType.DMA((2 * count,)),
            pltpu.SemaphoreType.DMA((2,)),
        ],
        compiler_params=BIG,
        cost_estimate=pl.CostEstimate(
            flops=8 * rows * depth * plan.wide, bytes_accessed=8 * depth * plan.both, transcendentals=0
        ),
        name="project",
    )(places, normed_low, grad_rows, *blocks)


def attend_kernel(
    plan, key_label_ref, query_label_ref, query_ref, key_ref, value_ref, mixed_grad_ref,
    mixed_ref, query_grad_ref, key_grad_ref, value_grad_ref, mixed_turned, query_turned, key_sum, value_sum,
):
    rows = query_ref.shape[0]
    padded = query_label_ref.shape[1]
    scale = HEAD_DIM ** (-0.5)
    fill = jnp.zeros((padded - rows, plan.wide), bf16)
    query = jnp.concatenate([query_ref[...], fill], axis=0)
    mixed_grad = jnp.concatenate([mixed_grad_ref[...], fill], axis=0)
    key_turned = jnp.concatenate([key_ref[...], fill], axis=0).T
    value_turned = jnp.concatenate([value_ref[...], fill], axis=0).T
    allowed = key_label_ref[...] == query_label_ref[...]
    mixed_turned[...] = jnp.zeros_like(mixed_turned)
    query_turned[...] = jnp.zeros_like(query_turned)
    key_sum[...] = jnp.zeros_like(key_sum)
    value_sum[...] = jnp.zeros_like(value_sum)
    zero = jnp.zeros((), bf16)
    for head in range(plan.heads):
        a, b, low, high = plan.window(head, 0)
        c, d, low_v, high_v = plan.window(head, plan.base)
        lane = a + lax.broadcasted_iota(jnp.int32, (1, b - a), 1)
        lane_v = c + lax.broadcasted_iota(jnp.int32, (1, d - c), 1)
        here = (lane >= low) & (lane < high)
        here_v = (lane_v >= low_v) & (lane_v < high_v)
        queries = jnp.where(here, query[:, a:b], zero)
        grads = jnp.where(here_v, mixed_grad[:, c:d], zero)
        scores = jnp.where(allowed, nt_dot(key_ref[:, a:b], queries) * scale, -1e30)
        raised = jnp.exp(scores - jnp.max(scores, axis=0, keepdims=True))
        prob = raised * (1.0 / jnp.sum(raised, axis=0, keepdims=True))
        prob_half = prob.astype(bf16)
        prob_grad = nt_dot(value_ref[:, c:d], grads)
        delta = jnp.sum(prob * prob_grad, axis=0, keepdims=True)
        score_grad = (prob * (prob_grad - delta) * scale).astype(bf16)
        row = a + lax.broadcasted_iota(jnp.int32, (b - a, 1), 0)
        row_v = c + lax.broadcasted_iota(jnp.int32, (d - c, 1), 0)
        mixed_part = nn_dot(value_turned[c:d, :rows], prob_half)
        mixed_turned[c:d, :] += jnp.where((row_v >= low_v) & (row_v < high_v), mixed_part, 0.0)
        query_part = nn_dot(key_turned[a:b, :rows], score_grad)
        query_turned[a:b, :] += jnp.where((row >= low) & (row < high), query_part, 0.0)
        value_sum[:, c:d] += nn_dot(prob_half, grads)
        key_sum[:, a:b] += nn_dot(score_grad, queries)
    mixed_ref[...] = mixed_turned[...].T.astype(bf16)
    query_grad_ref[...] = query_turned[...].T.astype(bf16)
    key_grad_ref[...] = jnp.concatenate([key_sum[...].astype(bf16), fill], axis=0)
    value_grad_ref[...] = jnp.concatenate([value_sum[...].astype(bf16), fill], axis=0)


def attend(plan, key_labels, query_labels, query, key, value, mixed_grad):
    rows = query.shape[0]
    padded = query_labels.shape[1]
    out = jax.ShapeDtypeStruct((padded, plan.wide), bf16)
    return pl.pallas_call(
        functools.partial(attend_kernel, plan),
        out_shape=[out] * 4,
        in_specs=[WHOLE] * 6,
        out_specs=[WHOLE] * 4,
        scratch_shapes=[
            pltpu.VMEM((plan.wide, padded), f32),
            pltpu.VMEM((plan.wide, padded), f32),
            pltpu.VMEM((rows, plan.wide), f32),
            pltpu.VMEM((rows, plan.wide), f32),
        ],
        compiler_params=BIG,
        cost_estimate=pl.CostEstimate(
            flops=16 * plan.heads * rows * padded * LANES,
            bytes_accessed=16 * rows * plan.wide,
            transcendentals=plan.heads * rows * padded,
        ),
        name="attend",
    )(key_labels, query_labels, query, key, value, mixed_grad)


def weight_grad_kernel(
    plan, tables, normed_ref, grad_ref, mixed_ref, query_grad_ref, key_grad_ref, value_grad_ref, *rest
):
    sets = len(tables)
    place_refs, rest = rest[:sets], rest[sets:]
    outs, rest = rest[: 2 * sets], rest[2 * sets :]
    held = rest[:2]
    sems = rest[2]
    split, wide = plan.start, plan.wide
    depth = normed_ref.shape[0]
    step = depth // 4
    for at in range(4):
        here = slice(at * step, (at + 1) * step)
        for pair, (first, second, second_left) in enumerate(
            ((query_grad_ref, mixed_ref, grad_ref), (key_grad_ref, value_grad_ref, normed_ref))
        ):
            left = nn_dot(normed_ref[here, :], first[...])
            right = nn_dot(second_left[here, :], second[...])
            seam = left[:, split:wide] + right[:, : wide - split]
            held[pair][here, :split] = left[:, :split].astype(bf16)
            held[pair][here, split:wide] = seam.astype(bf16)
            held[pair][here, wide:] = right[:, wide - split :].astype(bf16)
    copies = []
    for number, (count, rows) in enumerate(tables):
        for pair in range(2):
            for at in range(count):
                first = place_refs[number][at] * rows
                if rows % 16 == 0:
                    first = pl.multiple_of(first, 16)
                copy = pltpu.make_async_copy(
                    held[pair].at[pl.ds(first, rows)], outs[2 * number + pair].at[at], sems.at[len(copies)]
                )
                copy.start()
                copies.append(copy)
    for copy in copies:
        copy.wait()


def weight_grads(plan, normed_turned, grad_turned, mixed, query_grad, key_grad, value_grad, places, rows):
    depth, padded = normed_turned.shape
    tables = tuple((place.shape[0], rows) for place in places)
    out = [jax.ShapeDtypeStruct((count, rows, plan.both), bf16) for count, rows in tables for _ in range(2)]
    return pl.pallas_call(
        functools.partial(weight_grad_kernel, plan, tables),
        out_shape=out,
        in_specs=[WHOLE] * 6 + [SCALARS] * len(places),
        out_specs=[ANYWHERE] * len(out),
        scratch_shapes=[
            pltpu.VMEM((depth, plan.both), bf16),
            pltpu.VMEM((depth, plan.both), bf16),
            pltpu.SemaphoreType.DMA((2 * sum(count for count, _ in tables),)),
        ],
        compiler_params=BIG,
        cost_estimate=pl.CostEstimate(
            flops=8 * depth * padded * plan.wide, bytes_accessed=4 * depth * plan.both, transcendentals=0
        ),
        name="weight_grads",
    )(normed_turned, grad_turned, mixed, query_grad, key_grad, value_grad, *places)


def finish_kernel(plan, sides, *rest):
    weights, rest = rest[:4], rest[4:]
    mixed, query, key, value = (rest[2 * at : 2 * at + 2] for at in range(4))
    normed_ref, inverse_ref, gain_ref, out_ref, part_ref, gain_part_ref, bias_part_ref, held = rest[8:]
    rows = normed_ref.shape[0]
    side = pl.program_id(0)
    left, right = slice(0, plan.wide), slice(plan.start, plan.both)
    out_sum = jnp.zeros(out_ref.shape[1:], f32)
    grad_sum = jnp.zeros(out_ref.shape[1:], f32)
    for chunk in range(2):
        qo_ref, kv_ref = weights[2 * chunk], weights[2 * chunk + 1]
        out_sum += nt_dot(mixed[chunk][:rows, :], qo_ref[:, right])
        grad_sum += nt_dot(query[chunk][:rows, :], qo_ref[:, left])
        grad_sum += nt_dot(key[chunk][:rows, :], kv_ref[:, left])
        grad_sum += nt_dot(value[chunk][:rows, :], kv_ref[:, right])
    out_ref[0] = out_sum.astype(bf16)
    held[side] = grad_sum

    @pl.when(side == sides - 1)
    def _():
        width = held.shape[2]
        total = sides * width
        mean_a = jnp.zeros((rows, 1), f32)
        mean_b = jnp.zeros((rows, 1), f32)
        for at in range(sides):
            here = slice(at * width, (at + 1) * width)
            grad = held[at]
            normed = normed_ref[:, here]
            gain_part_ref[:, here] = jnp.sum(grad * normed, axis=0, keepdims=True)
            bias_part_ref[:, here] = jnp.sum(grad, axis=0, keepdims=True)
            scaled = grad * gain_ref[:, here]
            mean_a += jnp.sum(scaled, axis=1, keepdims=True)
            mean_b += jnp.sum(scaled * normed, axis=1, keepdims=True)
        mean_a = mean_a / total
        mean_b = mean_b / total
        for at in range(sides):
            here = slice(at * width, (at + 1) * width)
            scaled = held[at] * gain_ref[:, here]
            part = inverse_ref[...] * (scaled - mean_a - normed_ref[:, here] * mean_b)
            part_ref[at] = part.astype(bf16)


def finish(plan, weights, mixed, query_grads, key_grads, value_grads, normed, inverse, gain, sides):
    rows, depth = normed.shape
    width = depth // sides
    return pl.pallas_call(
        functools.partial(finish_kernel, plan, sides),
        grid=(sides,),
        out_shape=[
            jax.ShapeDtypeStruct((sides, rows, width), bf16),
            jax.ShapeDtypeStruct((sides, rows, width), bf16),
            jax.ShapeDtypeStruct((1, depth), f32),
            jax.ShapeDtypeStruct((1, depth), f32),
        ],
        in_specs=[pl.BlockSpec((width, plan.both), lambda side: (side, 0))] * 4 + [WHOLE] * 11,
        out_specs=[pl.BlockSpec((1, rows, width), lambda side: (side, 0, 0))] + [WHOLE] * 3,
        scratch_shapes=[pltpu.VMEM((sides, rows, width), f32)],
        compiler_params=BIG,
        cost_estimate=pl.CostEstimate(
            flops=16 * rows * depth * plan.wide, bytes_accessed=8 * depth * plan.both, transcendentals=0
        ),
        name="finish",
    )(*weights, *mixed, *query_grads, *key_grads, *value_grads, normed, inverse, gain[None, :])


def adam_kernel(plan, scale, *refs):
    grads, (master, first, second), outs = refs[:4], refs[4:7], refs[7:]
    half = plan.kind
    for kind, (pair, side) in enumerate(((0, 0), (1, 0), (1, 1), (0, 1))):
        parts = [grads[2 * chunk + pair][:, side * half : (side + 1) * half] for chunk in range(2)]
        gradient = jnp.concatenate(parts, axis=1) * scale
        new = adam_update(master[:, kind, :], first[:, kind, :], second[:, kind, :], gradient, decay_rate)
        for out, value in zip(outs, new):
            out[:, kind, :] = value


def adam(plan, scale, grads, master, first, second):
    return pl.pallas_call(
        functools.partial(adam_kernel, plan, scale),
        out_shape=[jax.ShapeDtypeStruct(master.shape, f32)] * 3,
        in_specs=[WHOLE] * 7,
        out_specs=[WHOLE] * 3,
        compiler_params=BIG,
        name="adam",
    )(*grads, master, first, second)


def ring_of(chips):
    return list(range(0, chips, 2)) + list(range(chips - 1, 0, -2))


class Ring:
    def __init__(self, devices):
        self.chips = devices // 2
        walk = ring_of(self.chips)
        self.moves, self.swap = [], [(device, device ^ 1) for device in range(devices)]
        for at, chip in enumerate(walk):
            self.moves.append((2 * chip, 2 * walk[(at + 1) % self.chips]))
            self.moves.append((2 * chip + 1, 2 * walk[(at - 1) % self.chips] + 1))
        place = {chip: at for at, chip in enumerate(walk)}
        self.arrive, self.mine, self.other = [], [], []
        for device in range(devices):
            at, core = place[device // 2], device % 2

            def come(core, step):
                return 2 * walk[(at + (step if core else -step)) % self.chips] + core

            def leave(core, step):
                return 2 * walk[(at + (1 + step if core else -1 - step)) % self.chips] + core

            steps = range(self.chips)
            self.arrive.append([come(c, s) for s in steps for c in (core, 1 - core)])
            self.mine.append([leave(core, s) for s in steps])
            self.other.append([leave(1 - core, s) for s in steps])

    def row(self, table):
        return jnp.asarray(table, jnp.int32)[lax.axis_index("dp")]

    def gather(self, block):
        blocks = []
        for step in range(self.chips):
            blocks += [block, lax.ppermute(block, "dp", self.swap)]
            if step + 1 < self.chips:
                block = lax.ppermute(block, "dp", self.moves)
        return blocks

    def reduce(self, mine, other):
        near = lax.ppermute(other, "dp", self.swap)
        total = mine[0].astype(f32) + near[0].astype(f32)
        for step in range(1, self.chips):
            total = lax.ppermute(total.astype(bf16), "dp", self.moves).astype(f32)
            total = total + (mine[step].astype(f32) + near[step].astype(f32))
        return total


def sum_over_all(values, axes):
    for axis in axes:
        size = lax.axis_size(axis)
        if size & (size - 1):
            values = lax.psum(values, axis)
            continue
        reach = 1
        while reach < size:
            swap = [(at, at ^ reach) for at in range(size)]
            values = values + lax.ppermute(values, axis, swap)
            reach *= 2
    return values


def shards(
    tokens,
    cotangent,
    master,
    moment_one,
    moment_two,
    ln_gain,
    ln_bias,
    norm_moment_one,
    norm_moment_two,
    image_count,
    tokens_per_image,
):
    groups = lax.axis_size("dp")
    sides = lax.axis_size("mp")
    side = lax.axis_index("mp")
    plan = Plan(master.shape[2])
    shard_rows = master.shape[0]
    depth = shard_rows * groups
    rows, width = tokens.shape
    padded = round_up(rows, LANES)
    around = shard_rows % 16 == 0 and groups % 4 == 0
    swap_sides = [(at, at ^ 1) for at in range(sides)]

    packed = pack(plan, master)
    if around:
        ring = Ring(groups)
        blocks = [ring.gather(block) for block in packed]
        places = ring.row(ring.arrive)
        leave = [ring.row(ring.mine), ring.row(ring.other)]
        leave_rows = shard_rows
    else:
        blocks = [[lax.all_gather(block, "dp", axis=0, tiled=True)] for block in packed]
        places = jnp.zeros((1,), jnp.int32)
        leave = [places]
        leave_rows = depth

    other_tokens = lax.ppermute(tokens, "mp", swap_sides)
    other_cot = lax.ppermute(cotangent, "mp", swap_sides)

    def in_order(here, there):
        return jnp.concatenate([jnp.where(side == 0, here, there), jnp.where(side == 0, there, here)], axis=1)

    normed, inverse, normed_low = layer_norm(in_order(tokens, other_tokens), ln_gain, ln_bias)
    spots = jnp.arange(padded, dtype=jnp.int32)
    live = spots < image_count[0] * tokens_per_image[0]
    labels = jnp.where(live, spots // tokens_per_image[0], jnp.int32(-1))
    live_column = live[:rows, None]
    key_labels = labels[:rows, None]
    query_labels = jnp.where(spots < rows, labels, jnp.int32(-2))[None, :]
    grad_rows = jnp.where(live_column, in_order(cotangent, other_cot), jnp.zeros((), bf16))
    fill = ((0, padded - rows), (0, 0))
    normed_turned = jnp.pad(normed_low, fill).T
    grad_turned = jnp.pad(grad_rows, fill).T

    weights, mixed, query_grads, key_grads, value_grads, totals = [], [], [], [], [], []
    for chunk in range(2):
        query, key, value, mixed_grad, *full = project(
            plan, places, normed_low, grad_rows, blocks[2 * chunk] + blocks[2 * chunk + 1]
        )
        weights += full
        grads = attend(plan, key_labels, query_labels, query, key, value, mixed_grad)
        for held, one in zip((mixed, query_grads, key_grads, value_grads), grads):
            held.append(one)
        parts = weight_grads(plan, normed_turned, grad_turned, *grads, leave, leave_rows)
        for pair in range(2):
            if around:
                totals.append(ring.reduce(parts[pair], parts[2 + pair]))
            else:
                total = lax.psum_scatter(parts[pair][0], "dp", scatter_dimension=0, tiled=True)
                totals.append(total.astype(f32))

    out_parts, input_parts, gain_part, bias_part = finish(
        plan, weights, mixed, query_grads, key_grads, value_grads, normed, inverse, ln_gain, sides
    )

    def across(parts):
        away = lax.ppermute(parts[1 - side], "mp", swap_sides)
        return parts[side].astype(f32) + away.astype(f32)

    block_out = (tokens.astype(f32) + across(out_parts)).astype(bf16)
    grad_local = jnp.where(live_column, cotangent, jnp.zeros((), bf16))
    input_grad = (grad_local.astype(f32) + across(input_parts)).astype(bf16)

    norm_param_grad = sum_over_all(jnp.concatenate([gain_part, bias_part]), ("dp", "mp")) / groups
    new_norm, new_norm_moment_one, new_norm_moment_two = adam_update(
        jnp.stack([ln_gain, ln_bias]), norm_moment_one, norm_moment_two, norm_param_grad, 0.0
    )
    new_master, new_moment_one, new_moment_two = adam(
        plan, 1.0 / groups, totals, master, moment_one, moment_two
    )
    return (
        block_out,
        input_grad,
        new_master,
        new_moment_one,
        new_moment_two,
        new_norm[0],
        new_norm[1],
        new_norm_moment_one,
        new_norm_moment_two,
    )


def solution(mesh):
    rows = P("dp", "mp")
    cube = P("dp", None, "mp")
    return jax.shard_map(
        shards,
        mesh=mesh,
        in_specs=(rows, rows, cube, cube, cube, P(), P(), P(), P(), P("dp"), P("dp")),
        out_specs=(rows, rows, cube, cube, cube, P(), P(), P(), P()),
        check_vma=False,
    )
```

```python
import functools

import jax
import jax.numpy as jnp
from jax import lax
from jax.experimental import pallas as pl
from jax.experimental.pallas import tpu as pltpu
from jax.sharding import PartitionSpec as P

HEAD_DIM = 112
LANES = 128

eps_norm = 1e-06
beta_one = 0.9
beta_two = 0.95
learn_rate = 0.01
decay_rate = 0.1
adam_eps = 1e-08
step_count = 10.0

bf16 = jnp.bfloat16
f32 = jnp.float32
WHOLE = pl.BlockSpec(memory_space=pltpu.VMEM)
SCALARS = pl.BlockSpec(memory_space=pltpu.SMEM)
ANYWHERE = pl.BlockSpec(memory_space=pl.ANY)


def room(size):
    return pltpu.CompilerParams(vmem_limit_bytes=size * 1024 * 1024)


def cost(flops, size, exps=0):
    return pl.CostEstimate(flops=flops, bytes_accessed=size, transcendentals=exps)


def round_up(value, unit):
    return -(-value // unit) * unit


def nt_dot(left, right):
    return lax.dot_general(left, right, (((1,), (1,)), ((), ())), preferred_element_type=f32)


def tn_dot(left, right):
    return lax.dot_general(left, right, (((0,), (0,)), ((), ())), preferred_element_type=f32)


def nn_dot(left, right):
    return jnp.dot(left, right, preferred_element_type=f32)


def adam_update(weight_now, moment_first, moment_second, gradient, decay):
    first_new = beta_one * moment_first + (1.0 - beta_one) * gradient
    second_new = beta_two * moment_second + (1.0 - beta_two) * gradient * gradient
    first_hat = first_new / (1.0 - beta_one**step_count)
    second_hat = second_new / (1.0 - beta_two**step_count)
    weight_new = weight_now - learn_rate * (
        first_hat / (jnp.sqrt(second_hat) + adam_eps) + decay * weight_now
    )
    return (weight_new, first_new, second_new)


class Plan:
    def __init__(self, columns):
        self.kind = columns // 2
        self.both = 2 * self.kind
        self.start = self.kind // LANES * LANES
        self.base = self.kind - self.start
        self.wide = self.both - self.start
        self.heads = self.kind // HEAD_DIM

    def window(self, head, base):
        low = base + head * HEAD_DIM
        high = low + HEAD_DIM
        return (low // LANES * LANES, min(self.wide, round_up(high, LANES)), low, high)


def pack_kernel(plan, master_ref, *outs):
    for chunk in range(2):
        for pair, kinds in enumerate(((0, 3), (1, 2))):
            columns = [
                master_ref[:, kind, chunk * plan.kind : (chunk + 1) * plan.kind] for kind in kinds
            ]
            outs[2 * chunk + pair][...] = jnp.concatenate(columns, axis=1).astype(bf16)


def pack(plan, master):
    out = jax.ShapeDtypeStruct((master.shape[0], plan.both), bf16)
    return pl.pallas_call(
        functools.partial(pack_kernel, plan),
        out_shape=[out] * 4,
        in_specs=[WHOLE],
        out_specs=[WHOLE] * 4,
        compiler_params=room(12),
        name="pack",
    )(master)


def in_order(side, here, there):
    return (jnp.where(side == 0, here, there), jnp.where(side == 0, there, here))


def norm_kernel(side_ref, here_ref, there_ref, gain_ref, bias_ref, low_ref, center_ref, inverse_ref):
    halves = [half.astype(f32) for half in in_order(side_ref[0], here_ref[...], there_ref[...])]
    width = here_ref.shape[1]
    total = 2 * width
    center = sum(jnp.sum(half, axis=1, keepdims=True) for half in halves) / total
    shifted = [half - center for half in halves]
    spread = sum(jnp.sum(half * half, axis=1, keepdims=True) for half in shifted) / total
    inverse = lax.rsqrt(spread + eps_norm)
    center_ref[...] = center
    inverse_ref[...] = inverse
    for at, half in enumerate(shifted):
        here = slice(at * width, (at + 1) * width)
        low_ref[:, here] = (half * inverse * gain_ref[:, here] + bias_ref[:, here]).astype(bf16)


def norm(side, here, there, gain, bias):
    rows, width = here.shape
    column = jax.ShapeDtypeStruct((rows, 1), f32)
    return pl.pallas_call(
        norm_kernel,
        out_shape=[jax.ShapeDtypeStruct((rows, 2 * width), bf16), column, column],
        in_specs=[SCALARS] + [WHOLE] * 4,
        out_specs=[WHOLE] * 3,
        compiler_params=room(16),
        cost_estimate=cost(0, 8 * rows * width),
        name="norm",
    )(side, here, there, gain, bias)


def live_kernel(side_ref, image_ref, here_ref, there_ref, out_ref):
    rows, width = here_ref.shape
    spot = lax.broadcasted_iota(jnp.int32, (rows, 1), 0)
    live = spot < image_ref[0] * image_ref[1]
    for at, half in enumerate(in_order(side_ref[0], here_ref[...], there_ref[...])):
        out_ref[:, at * width : (at + 1) * width] = jnp.where(live, half, jnp.zeros((), bf16))


def live_rows(side, image, here, there):
    rows, width = here.shape
    return pl.pallas_call(
        live_kernel,
        out_shape=jax.ShapeDtypeStruct((rows, 2 * width), bf16),
        in_specs=[SCALARS] * 2 + [WHOLE] * 2,
        out_specs=WHOLE,
        compiler_params=room(16),
        cost_estimate=cost(0, 8 * rows * width),
        name="live_rows",
    )(side, image, here, there)


def copies_of(blocks, places, held, sems):
    copies = []
    for at, block in enumerate(blocks):
        rows = block.shape[0]
        first = places[at] * rows
        if rows % 16 == 0:
            first = pl.multiple_of(first, 16)
        copies.append(pltpu.make_async_copy(block, held.at[pl.ds(first, rows)], sems.at[at]))
        copies[-1].start()
    return copies


def project_kernel(plan, count, masked, place_ref, left_ref, right_ref, *rest):
    blocks, (first_ref, second_ref, full, held, sems, out_sem) = rest[:count], rest[count:]
    for copy in copies_of(blocks, place_ref, held, sems):
        copy.wait()
    keep = pltpu.make_async_copy(held, full, out_sem)
    keep.start()
    first_ref[...] = nn_dot(left_ref[...], held[:, : plan.wide]).astype(bf16)
    second = nn_dot(right_ref[...], held[:, plan.start :])
    if masked:
        live = lax.broadcasted_iota(jnp.int32, (1, plan.wide), 1) >= plan.base
        second = jnp.where(live, second, 0.0)
    second_ref[...] = second.astype(bf16)
    keep.wait()


def project(plan, masked, places, left, right, blocks):
    count = len(blocks)
    rows, depth = left.shape
    out = jax.ShapeDtypeStruct((rows, plan.wide), bf16)
    return pl.pallas_call(
        functools.partial(project_kernel, plan, count, masked),
        out_shape=[out, out, jax.ShapeDtypeStruct((depth, plan.both), bf16)],
        in_specs=[SCALARS, WHOLE, WHOLE] + [ANYWHERE] * count,
        out_specs=[WHOLE, WHOLE, ANYWHERE],
        scratch_shapes=[
            pltpu.VMEM((depth, plan.both), bf16),
            pltpu.SemaphoreType.DMA((count,)),
            pltpu.SemaphoreType.DMA(()),
        ],
        compiler_params=room(20),
        cost_estimate=cost(4 * rows * depth * plan.wide, 4 * depth * plan.both),
        name="project",
    )(places, left, right, *blocks)


def label(spot, live, length):
    at = ((spot.astype(f32) + 0.5) / length.astype(f32)).astype(jnp.int32)
    return jnp.where(spot < live, at, -1)


def attend_kernel(
    plan, image_ref, query_ref, key_ref, value_ref, mixed_grad_ref,
    mixed_ref, query_grad_ref, key_grad_ref, value_grad_ref, mixed_turned, query_turned, key_sum, value_sum,
):
    rows = query_ref.shape[0]
    padded = mixed_turned.shape[1]
    scale = HEAD_DIM ** (-0.5)
    fill = jnp.zeros((padded - rows, plan.wide), bf16)
    query = jnp.concatenate([query_ref[...], fill], axis=0)
    mixed_grad = jnp.concatenate([mixed_grad_ref[...], fill], axis=0)
    key_turned = jnp.concatenate([key_ref[...], fill], axis=0).T
    value_turned = jnp.concatenate([value_ref[...], fill], axis=0).T
    live = image_ref[0] * image_ref[1]
    key_spot = lax.broadcasted_iota(jnp.int32, (rows, 1), 0)
    query_spot = lax.broadcasted_iota(jnp.int32, (1, padded), 1)
    length = jnp.full((1, 1), image_ref[1], jnp.int32)
    query_label = jnp.where(query_spot < rows, label(query_spot, live, length), -2)
    allowed = label(key_spot, live, length) == query_label
    mixed_turned[...] = jnp.zeros_like(mixed_turned)
    query_turned[...] = jnp.zeros_like(query_turned)
    key_sum[...] = jnp.zeros_like(key_sum)
    value_sum[...] = jnp.zeros_like(value_sum)
    zero = jnp.zeros((), bf16)
    for head in range(plan.heads):
        a, b, low, high = plan.window(head, 0)
        c, d, low_v, high_v = plan.window(head, plan.base)
        lane = a + lax.broadcasted_iota(jnp.int32, (1, b - a), 1)
        lane_v = c + lax.broadcasted_iota(jnp.int32, (1, d - c), 1)
        here = (lane >= low) & (lane < high)
        here_v = (lane_v >= low_v) & (lane_v < high_v)
        queries = jnp.where(here, query[:, a:b], zero)
        grads = jnp.where(here_v, mixed_grad[:, c:d], zero)
        scores = jnp.where(allowed, nt_dot(key_ref[:, a:b], queries) * scale, -1e30)
        raised = jnp.exp(scores - jnp.max(scores, axis=0, keepdims=True))
        prob = raised * (1.0 / jnp.sum(raised, axis=0, keepdims=True))
        prob_half = prob.astype(bf16)
        prob_grad = nt_dot(value_ref[:, c:d], grads)
        delta = jnp.sum(prob * prob_grad, axis=0, keepdims=True)
        score_grad = (prob * (prob_grad - delta) * scale).astype(bf16)
        row = a + lax.broadcasted_iota(jnp.int32, (b - a, 1), 0)
        row_v = c + lax.broadcasted_iota(jnp.int32, (d - c, 1), 0)
        mixed_part = nn_dot(value_turned[c:d, :rows], prob_half)
        mixed_turned[c:d, :] += jnp.where((row_v >= low_v) & (row_v < high_v), mixed_part, 0.0)
        query_part = nn_dot(key_turned[a:b, :rows], score_grad)
        query_turned[a:b, :] += jnp.where((row >= low) & (row < high), query_part, 0.0)
        value_sum[:, c:d] += nn_dot(prob_half, grads)
        key_sum[:, a:b] += nn_dot(score_grad, queries)
    mixed_ref[...] = mixed_turned[...].T[:rows].astype(bf16)
    query_grad_ref[...] = query_turned[...].T[:rows].astype(bf16)
    key_grad_ref[...] = key_sum[...].astype(bf16)
    value_grad_ref[...] = value_sum[...].astype(bf16)


def attend(plan, image, query, key, value, mixed_grad):
    rows = query.shape[0]
    padded = round_up(rows, LANES)
    out = jax.ShapeDtypeStruct((rows, plan.wide), bf16)
    return pl.pallas_call(
        functools.partial(attend_kernel, plan),
        out_shape=[out] * 4,
        in_specs=[SCALARS] + [WHOLE] * 4,
        out_specs=[WHOLE] * 4,
        scratch_shapes=[
            pltpu.VMEM((plan.wide, padded), f32),
            pltpu.VMEM((plan.wide, padded), f32),
            pltpu.VMEM((rows, plan.wide), f32),
            pltpu.VMEM((rows, plan.wide), f32),
        ],
        compiler_params=room(24),
        cost_estimate=cost(
            16 * plan.heads * rows * padded * LANES, 16 * rows * plan.wide, plan.heads * rows * padded
        ),
        name="attend",
    )(image, query, key, value, mixed_grad)


def weight_grad_kernel(plan, sizes, rows, *refs):
    place_refs, refs = refs[: len(sizes)], refs[len(sizes) :]
    (left_ref, right_ref, first_ref, second_ref), refs = refs[:4], refs[4:]
    outs, (held, sems) = refs[: len(sizes)], refs[len(sizes) :]
    split, wide = plan.start, plan.wide
    depth = left_ref.shape[1]
    for at in range(2):
        here = slice(at * depth // 2, (at + 1) * depth // 2)
        left = tn_dot(left_ref[:, here], first_ref[...])
        right = tn_dot(right_ref[:, here], second_ref[...])
        held[here, :split] = left[:, :split].astype(bf16)
        held[here, split:wide] = (left[:, split:wide] + right[:, : wide - split]).astype(bf16)
        held[here, wide:] = right[:, wide - split :].astype(bf16)
    copies = []
    for places, size, out in zip(place_refs, sizes, outs):
        for at in range(size):
            first = places[at] * rows
            if rows % 16 == 0:
                first = pl.multiple_of(first, 16)
            copies.append(
                pltpu.make_async_copy(held.at[pl.ds(first, rows)], out.at[at], sems.at[len(copies)])
            )
            copies[-1].start()
    for copy in copies:
        copy.wait()


def weight_grads(plan, places, rows, left, right, first, second):
    depth = left.shape[1]
    sizes = tuple(place.shape[0] for place in places)
    return pl.pallas_call(
        functools.partial(weight_grad_kernel, plan, sizes, rows),
        out_shape=[jax.ShapeDtypeStruct((size, rows, plan.both), bf16) for size in sizes],
        in_specs=[SCALARS] * len(sizes) + [WHOLE] * 4,
        out_specs=[ANYWHERE] * len(sizes),
        scratch_shapes=[
            pltpu.VMEM((depth, plan.both), bf16),
            pltpu.SemaphoreType.DMA((sum(sizes),)),
        ],
        compiler_params=room(24),
        cost_estimate=cost(4 * depth * left.shape[0] * plan.wide, 4 * depth * plan.both),
        name="weight_grads",
    )(*places, left, right, first, second)


def out_kernel(plan, *refs):
    weights, mixed, out_ref = refs[:2], refs[2:4], refs[4]
    out_ref[0] = sum(
        nt_dot(rows[...], weight[:, plan.start :]) for rows, weight in zip(mixed, weights)
    ).astype(bf16)


def out_parts(plan, weights, mixed, sides):
    rows = mixed[0].shape[0]
    depth = weights[0].shape[0]
    width = depth // sides
    return pl.pallas_call(
        functools.partial(out_kernel, plan),
        grid=(sides,),
        out_shape=jax.ShapeDtypeStruct((sides, rows, width), bf16),
        in_specs=[pl.BlockSpec((width, plan.both), lambda at: (at, 0))] * 2 + [WHOLE] * 2,
        out_specs=pl.BlockSpec((1, rows, width), lambda at: (at, 0, 0)),
        compiler_params=room(20),
        cost_estimate=cost(4 * rows * depth * plan.wide, 4 * depth * plan.both),
        name="out_parts",
    )(*weights, *mixed)


def norm_grad_kernel(plan, sides, side_ref, *refs):
    weights, grads, refs = refs[:4], refs[4:10], refs[10:]
    here_ref, there_ref, center_ref, inverse_ref, gain_ref, part_ref, sums_ref, held = refs
    step = pl.program_id(0)
    left, right = slice(0, plan.wide), slice(plan.start, plan.both)
    total = jnp.zeros(held.shape[1:], f32)
    for chunk in range(2):
        query, key, value = grads[3 * chunk : 3 * chunk + 3]
        qo, kv = weights[2 * chunk : 2 * chunk + 2]
        total += nt_dot(query[...], qo[:, left])
        total += nt_dot(key[...], kv[:, left])
        total += nt_dot(value[...], kv[:, right])
    held[step] = total

    @pl.when(step == sides - 1)
    def _():
        width = held.shape[2]
        center, inverse = center_ref[...], inverse_ref[...]
        halves = in_order(side_ref[0], here_ref[...], there_ref[...])
        normed = [(half.astype(f32) - center) * inverse for half in halves]
        mean_a, mean_b = 0.0, 0.0
        for at in range(sides):
            here = slice(at * width, (at + 1) * width)
            grad = held[at]
            product = grad * normed[at]
            sums_ref[0:1, here] = jnp.sum(product, axis=0, keepdims=True)
            sums_ref[1:2, here] = jnp.sum(grad, axis=0, keepdims=True)
            mean_a += jnp.sum(grad * gain_ref[:, here], axis=1, keepdims=True)
            mean_b += jnp.sum(product * gain_ref[:, here], axis=1, keepdims=True)
        mean_a = mean_a / (sides * width)
        mean_b = mean_b / (sides * width)
        for at in range(sides):
            scaled = held[at] * gain_ref[:, at * width : (at + 1) * width]
            part_ref[at] = (inverse * (scaled - mean_a - normed[at] * mean_b)).astype(bf16)


def norm_grads(plan, side, weights, grads, here, there, center, inverse, gain, sides):
    rows, width = here.shape
    depth = sides * width
    return pl.pallas_call(
        functools.partial(norm_grad_kernel, plan, sides),
        grid=(sides,),
        out_shape=[
            jax.ShapeDtypeStruct((sides, rows, width), bf16),
            jax.ShapeDtypeStruct((2, depth), f32),
        ],
        in_specs=[SCALARS]
        + [pl.BlockSpec((width, plan.both), lambda at: (at, 0))] * 4
        + [WHOLE] * 11,
        out_specs=[WHOLE] * 2,
        scratch_shapes=[pltpu.VMEM((sides, rows, width), f32)],
        compiler_params=room(40),
        cost_estimate=cost(12 * rows * depth * plan.wide, 8 * depth * plan.both),
        name="norm_grads",
    )(side, *weights, *grads, here, there, center, inverse, gain)


def adam_kernel(plan, counts, scale, first_block, held, *refs):
    terms, refs = refs[: sum(counts)], refs[sum(counts) :]
    (master, first, second), outs = refs[:3], refs[-3:]
    pairs, at = [], 0
    for count in counts:
        pairs.append(terms[at : at + count])
        at += count

    def columns(pair, low, high):
        return sum(term[0, :, low:high].astype(f32) for term in pairs[pair])

    def update(block):
        low, high = block * LANES, (block + 1) * LANES
        for kind, (pair, side) in enumerate(((0, 0), (1, 0), (1, 1), (0, 1))):
            parts = []
            for chunk in range(2):
                a, b = max(low, chunk * plan.kind), min(high, (chunk + 1) * plan.kind)
                if a < b:
                    move = (side - chunk) * plan.kind
                    parts.append(columns(2 * chunk + pair, a + move, b + move))
            gradient = (parts[0] if len(parts) == 1 else jnp.concatenate(parts, axis=1)) * scale
            new = adam_update(master[:, kind, :], first[:, kind, :], second[:, kind, :], gradient, decay_rate)
            for out, value in zip(outs, new):
                out[:, kind, :] = value

    step = pl.program_id(0)
    for at in range(held):
        pl.when(step == at)(functools.partial(update, first_block + at))


def adam(plan, scale, terms, states, first_block, blocks, so_far=()):
    rows = states[0].shape[0]
    flat = [(term, at) for one in terms for term, at in one]
    block = pl.BlockSpec((rows, 4, LANES), lambda step: (0, 0, first_block + step))
    return pl.pallas_call(
        functools.partial(adam_kernel, plan, tuple(len(one) for one in terms), scale, first_block, blocks),
        grid=(blocks,),
        out_shape=[jax.ShapeDtypeStruct(states[0].shape, f32)] * 3,
        in_specs=[pl.BlockSpec((1, rows, plan.both), lambda step, at=at: (at, 0, 0)) for _, at in flat]
        + [block] * 3
        + [ANYWHERE] * len(so_far),
        out_specs=[block] * 3,
        input_output_aliases={len(flat) + 3 + at: at for at in range(len(so_far))},
        compiler_params=room(24),
        cost_estimate=cost(0, 24 * rows * 4 * LANES * blocks),
        name="adam",
    )(*[term for term, _ in flat], *states, *so_far)


def ring_of(chips):
    return list(range(0, chips, 2)) + list(range(chips - 1, 0, -2))


class Ring:
    def __init__(self, devices):
        self.chips = devices // 2
        walk = ring_of(self.chips)
        self.moves, self.swap = [], [(device, device ^ 1) for device in range(devices)]
        for at, chip in enumerate(walk):
            self.moves.append((2 * chip, 2 * walk[(at + 1) % self.chips]))
            self.moves.append((2 * chip + 1, 2 * walk[(at - 1) % self.chips] + 1))
        place = {chip: at for at, chip in enumerate(walk)}
        self.arrive, self.mine, self.other = [], [], []
        for device in range(devices):
            at, core = place[device // 2], device % 2

            def come(core, step):
                return 2 * walk[(at + (step if core else -step)) % self.chips] + core

            def leave(core, step):
                return 2 * walk[(at + (1 + step if core else -1 - step)) % self.chips] + core

            steps = range(self.chips)
            self.arrive.append([come(c, s) for s in steps for c in (core, 1 - core)])
            self.mine.append([leave(core, s) for s in steps])
            self.other.append([leave(1 - core, s) for s in steps])

    def row(self):
        table = [a + m + o for a, m, o in zip(self.arrive, self.mine, self.other)]
        row = jnp.asarray(table, jnp.int32)[lax.axis_index("dp")]
        return jnp.split(row, [2 * self.chips, 3 * self.chips])


class Gather:
    def __init__(self, ring, block):
        self.ring, self.block, self.blocks = ring, block, []
        self.left = ring.chips - 1

    def hop(self, after):
        block = self.block = tie(self.block, after)
        if self.left:
            self.block = lax.ppermute(block, "dp", self.ring.moves)
        self.left -= 1
        self.blocks += [block, lax.ppermute(block, "dp", self.ring.swap)]
        return block


class Reduce:
    def __init__(self, ring, mine, other):
        self.ring, self.mine, self.step = ring, mine, 0
        self.near = lax.ppermute(other, "dp", ring.swap)
        self.total = self.add(0.0)
        self.left = ring.chips - 1

    def add(self, so_far):
        here = self.mine[self.step].astype(f32) + self.near[self.step].astype(f32)
        return (so_far + here).astype(bf16)

    def hop(self, after):
        sent = tie(self.total, after)
        self.come = lax.ppermute(sent, "dp", self.ring.moves)
        self.left -= 1
        self.step += 1
        self.total = self.add(self.come.astype(f32)) if self.left else self.come
        return sent

    def terms(self):
        return [(self.come[None], 0), (self.mine, self.step), (self.near, self.step)]


def tie(value, after):
    if after is None:
        return value
    return lax.optimization_barrier((value, after))[0]


def sum_over_all(values, axes):
    for axis in axes:
        size = lax.axis_size(axis)
        if size & (size - 1):
            values = lax.psum(values, axis)
            continue
        reach = 1
        while reach < size:
            swap = [(at, at ^ reach) for at in range(size)]
            values = values + lax.ppermute(values, axis, swap)
            reach *= 2
    return values


def shards(
    tokens,
    cotangent,
    master,
    moment_one,
    moment_two,
    ln_gain,
    ln_bias,
    norm_moment_one,
    norm_moment_two,
    image_count,
    tokens_per_image,
):
    groups = lax.axis_size("dp")
    sides = lax.axis_size("mp")
    side = lax.axis_index("mp")
    plan = Plan(master.shape[2])
    shard_rows = master.shape[0]
    depth = shard_rows * groups
    around = shard_rows % 16 == 0 and groups % 4 == 0
    swap_sides = [(at, at ^ 1) for at in range(sides)]
    side_now = side.astype(jnp.int32)[None]
    image = jnp.concatenate([image_count, tokens_per_image])
    gain, bias = ln_gain[None, :], ln_bias[None, :]

    packed = pack(plan, master)
    if around:
        ring = Ring(groups)
        arrive, *leave = ring.row()
        leave_rows = shard_rows
        chains = [Gather(ring, block) for block in packed]
    else:
        arrive = jnp.zeros((1,), jnp.int32)
        leave, leave_rows = [arrive], depth

    last = None

    def hop(*which):
        nonlocal last
        for chain in which:
            last = chain.hop(last)

    other_tokens = lax.ppermute(tokens, "mp", swap_sides)
    other_cot = lax.ppermute(tie(cotangent, other_tokens), "mp", swap_sides)

    def norm_now():
        return norm(side_now, tie(tokens, last), other_tokens, gain, bias)

    def live_now():
        return live_rows(side_now, image, tie(cotangent, last), other_cot)

    if around:
        first_a, first_b, second_a, second_b = chains
        hop(first_a, first_b, second_a)
        hop(first_a, first_b, second_b)
        hop(first_a, first_b, second_a)
        hop(first_a, first_b, second_b)
        normed_low, center, inverse = norm_now()
        hop(first_a, first_b, second_a)
        hop(first_a, first_b, second_b)
        grad_rows = live_now()
        hop(first_a, first_b, second_a, second_b)
        hop(first_a, first_b)
        blocks = [chain.blocks for chain in chains]
    else:
        normed_low, center, inverse = norm_now()
        grad_rows = live_now()
        blocks = [[lax.all_gather(block, "dp", axis=0, tiled=True)] for block in packed]

    def work(kernel, *args):
        nonlocal last
        args = list(args)
        args[0] = tie(args[0], last)
        outs = kernel(*args)
        last = outs[0]
        return outs

    def between(*which):
        if around:
            hop(*which)

    weights, mixed, grads = [], [], []

    def project_qo(chunk):
        return work(functools.partial(project, plan, True, arrive), normed_low, grad_rows, blocks[2 * chunk])

    def project_kv(chunk):
        return work(functools.partial(project, plan, False, arrive), normed_low, normed_low, blocks[2 * chunk + 1])

    def attend_now(query, key, value, mixed_grad):
        return work(lambda query, *rest: attend(plan, image, query, *rest), query, key, value, mixed_grad)

    def grads_now(*args):
        return work(functools.partial(weight_grads, plan, leave, leave_rows), *args)

    def reduced(parts):
        if around:
            return Reduce(ring, *parts)
        return lax.psum_scatter(parts[0], "dp", scatter_dimension=1, tiled=True)

    def terms(total):
        return total.terms() if around else [(total, 0)]

    if around:
        hop(second_a, second_b)
    query, mixed_grad, full_qo = project_qo(0)
    key, value, full_kv = project_kv(0)
    weights += [full_qo, full_kv]
    if around:
        hop(second_a, second_b)
    mixed_a, query_grad, key_grad, value_grad = attend_now(query, key, value, mixed_grad)
    grads += [query_grad, key_grad, value_grad]
    if around:
        hop(second_a, second_b)
    qo_a = reduced(grads_now(normed_low, grad_rows, query_grad, mixed_a))
    if around:
        hop(second_a, second_b)
    kv_a = reduced(grads_now(normed_low, normed_low, key_grad, value_grad))

    between(qo_a)
    query, mixed_grad, full_qo = project_qo(1)
    between(qo_a, kv_a)
    key, value, full_kv = project_kv(1)
    weights += [full_qo, full_kv]
    between(qo_a, kv_a)
    mixed_b, query_grad, key_grad, value_grad = attend_now(query, key, value, mixed_grad)
    grads += [query_grad, key_grad, value_grad]
    between(qo_a, kv_a)
    qo_b = reduced(grads_now(normed_low, grad_rows, query_grad, mixed_b))
    between(qo_a, kv_a)
    kv_b = reduced(grads_now(normed_low, normed_low, key_grad, value_grad))

    between(qo_a, kv_a, qo_b, kv_b)
    parts = work(
        lambda first, *rest: [out_parts(plan, weights[0::2], [first, *rest], sides)], mixed_a, mixed_b
    )[0]
    out_away = lax.ppermute(parts[1 - side], "mp", swap_sides)
    block_out = (tokens.astype(f32) + (parts[side].astype(f32) + out_away.astype(f32))).astype(bf16)
    between(qo_a, kv_a, qo_b, kv_b)
    parts, sums = work(
        lambda first, *rest: norm_grads(
            plan, side_now, weights, [first, *rest], tokens, other_tokens, center, inverse, gain, sides
        ),
        *grads,
    )
    input_away = lax.ppermute(tie(parts[1 - side], out_away), "mp", swap_sides)
    live = jnp.arange(tokens.shape[0])[:, None] < image_count[0] * tokens_per_image[0]
    grad_local = jnp.where(live, cotangent, jnp.zeros((), bf16))
    input_grad = (grad_local.astype(f32) + (parts[side].astype(f32) + input_away.astype(f32))).astype(bf16)
    norm_param_grad = sum_over_all(sums, ("dp", "mp")) / groups
    new_norm, new_norm_moment_one, new_norm_moment_two = adam_update(
        jnp.stack([ln_gain, ln_bias]), norm_moment_one, norm_moment_two, norm_param_grad, 0.0
    )

    between(kv_a, qo_b, kv_b)
    between(qo_b, kv_b)
    states = [master, moment_one, moment_two]
    whole_blocks = plan.kind // LANES
    all_blocks = master.shape[2] // LANES
    firsts = [terms(qo_a), terms(kv_a)]
    begun = work(
        lambda first, *rest: adam(plan, 1.0 / groups, firsts, [first, *rest], 0, whole_blocks), *states
    )
    for _ in range(3):
        between(qo_b, kv_b)
    new_master, new_moment_one, new_moment_two = adam(
        plan,
        1.0 / groups,
        firsts + [terms(qo_b), terms(kv_b)],
        states,
        whole_blocks,
        all_blocks - whole_blocks,
        begun,
    )
    return (
        block_out,
        input_grad,
        new_master,
        new_moment_one,
        new_moment_two,
        new_norm[0],
        new_norm[1],
        new_norm_moment_one,
        new_norm_moment_two,
    )


def solution(mesh):
    rows = P("dp", "mp")
    cube = P("dp", None, "mp")
    return jax.shard_map(
        shards,
        mesh=mesh,
        in_specs=(rows, rows, cube, cube, cube, P(), P(), P(), P(), P("dp"), P("dp")),
        out_specs=(rows, rows, cube, cube, cube, P(), P(), P(), P()),
        check_vma=False,
    )
```

```python
import functools

import jax
import jax.numpy as jnp
from jax import lax
from jax.experimental import pallas as pl
from jax.experimental.pallas import tpu as pltpu
from jax.sharding import PartitionSpec as P

HEAD_DIM = 112
LANES = 128

eps_norm = 1e-06
beta_one = 0.9
beta_two = 0.95
learn_rate = 0.01
decay_rate = 0.1
adam_eps = 1e-08
step_count = 10.0

bf16 = jnp.bfloat16
f32 = jnp.float32
WHOLE = pl.BlockSpec(memory_space=pltpu.VMEM)
SCALARS = pl.BlockSpec(memory_space=pltpu.SMEM)
ANYWHERE = pl.BlockSpec(memory_space=pl.ANY)


def room(size):
    return pltpu.CompilerParams(vmem_limit_bytes=size * 1024 * 1024)


def cost(flops, size, exps=0):
    return pl.CostEstimate(flops=flops, bytes_accessed=size, transcendentals=exps)


def round_up(value, unit):
    return -(-value // unit) * unit


def nt_dot(left, right):
    return lax.dot_general(left, right, (((1,), (1,)), ((), ())), preferred_element_type=f32)


def tn_dot(left, right):
    return lax.dot_general(left, right, (((0,), (0,)), ((), ())), preferred_element_type=f32)


def nn_dot(left, right):
    return jnp.dot(left, right, preferred_element_type=f32)


def adam_update(weight_now, moment_first, moment_second, gradient, decay):
    first_new = beta_one * moment_first + (1.0 - beta_one) * gradient
    second_new = beta_two * moment_second + (1.0 - beta_two) * gradient * gradient
    first_hat = first_new / (1.0 - beta_one**step_count)
    second_hat = second_new / (1.0 - beta_two**step_count)
    weight_new = weight_now - learn_rate * (
        first_hat / (jnp.sqrt(second_hat) + adam_eps) + decay * weight_now
    )
    return (weight_new, first_new, second_new)


class Plan:
    def __init__(self, columns):
        self.kind = columns // 2
        self.both = 2 * self.kind
        self.start = self.kind // LANES * LANES
        self.base = self.kind - self.start
        self.wide = self.both - self.start
        self.heads = self.kind // HEAD_DIM

    def window(self, head, base):
        low = base + head * HEAD_DIM
        high = low + HEAD_DIM
        return (low // LANES * LANES, min(self.wide, round_up(high, LANES)), low, high)


def pack_kernel(plan, master_ref, *outs):
    targets = [outs[0], outs[1], outs[2].at[0], outs[2].at[1]]
    for chunk in range(2):
        for pair, kinds in enumerate(((0, 3), (1, 2))):
            columns = [
                master_ref[:, kind, chunk * plan.kind : (chunk + 1) * plan.kind] for kind in kinds
            ]
            targets[2 * chunk + pair][...] = jnp.concatenate(columns, axis=1).astype(bf16)


def pack(plan, master):
    size = (master.shape[0], plan.both)
    return pl.pallas_call(
        functools.partial(pack_kernel, plan),
        out_shape=[jax.ShapeDtypeStruct(size, bf16)] * 2 + [jax.ShapeDtypeStruct((2, *size), bf16)],
        in_specs=[WHOLE],
        out_specs=[WHOLE] * 3,
        compiler_params=room(12),
        name="pack",
    )(master)


def in_order(side, here, there):
    return (jnp.where(side == 0, here, there), jnp.where(side == 0, there, here))


def norm_kernel(side_ref, here_ref, there_ref, gain_ref, bias_ref, low_ref, center_ref, inverse_ref):
    halves = [half.astype(f32) for half in in_order(side_ref[0], here_ref[...], there_ref[...])]
    width = here_ref.shape[1]
    total = 2 * width
    center = sum(jnp.sum(half, axis=1, keepdims=True) for half in halves) / total
    shifted = [half - center for half in halves]
    spread = sum(jnp.sum(half * half, axis=1, keepdims=True) for half in shifted) / total
    inverse = lax.rsqrt(spread + eps_norm)
    center_ref[...] = center
    inverse_ref[...] = inverse
    for at, half in enumerate(shifted):
        here = slice(at * width, (at + 1) * width)
        low_ref[:, here] = (half * inverse * gain_ref[:, here] + bias_ref[:, here]).astype(bf16)


def norm(side, here, there, gain, bias):
    rows, width = here.shape
    column = jax.ShapeDtypeStruct((rows, 1), f32)
    return pl.pallas_call(
        norm_kernel,
        out_shape=[jax.ShapeDtypeStruct((rows, 2 * width), bf16), column, column],
        in_specs=[SCALARS] + [WHOLE] * 4,
        out_specs=[WHOLE] * 3,
        compiler_params=room(16),
        cost_estimate=cost(0, 8 * rows * width),
        name="norm",
    )(side, here, there, gain, bias)


def live_kernel(side_ref, image_ref, here_ref, there_ref, out_ref):
    rows, width = here_ref.shape
    spot = lax.broadcasted_iota(jnp.int32, (rows, 1), 0)
    live = spot < image_ref[0] * image_ref[1]
    for at, half in enumerate(in_order(side_ref[0], here_ref[...], there_ref[...])):
        out_ref[:, at * width : (at + 1) * width] = jnp.where(live, half, jnp.zeros((), bf16))


def live_rows(side, image, here, there):
    rows, width = here.shape
    return pl.pallas_call(
        live_kernel,
        out_shape=jax.ShapeDtypeStruct((rows, 2 * width), bf16),
        in_specs=[SCALARS] * 2 + [WHOLE] * 2,
        out_specs=WHOLE,
        compiler_params=room(16),
        cost_estimate=cost(0, 8 * rows * width),
        name="live_rows",
    )(side, image, here, there)


def project_kernel(plan, count, apart, place_ref, normed_ref, grad_ref, *refs):
    blocks, (query_ref, mixed_grad_ref, key_ref, value_ref, *fulls) = refs[:-6], refs[-6:]
    normed = normed_ref[...]
    live = lax.broadcasted_iota(jnp.int32, (1, plan.wide), 1) >= plan.base
    for pair, full in enumerate(fulls):
        for at in range(count):
            block = blocks[pair * count + at] if apart else blocks[at].at[pair]
            rows = block.shape[0]
            first = place_ref[at] * rows
            if rows % 16 == 0:
                first = pl.multiple_of(first, 16)
            full[pl.ds(first, rows), :] = block[...]
        if pair == 0:
            query_ref[...] = nn_dot(normed, full[:, : plan.wide]).astype(bf16)
            mixed_grad = nn_dot(grad_ref[...], full[:, plan.start :])
            mixed_grad_ref[...] = jnp.where(live, mixed_grad, 0.0).astype(bf16)
        else:
            key_ref[...] = nn_dot(normed, full[:, : plan.wide]).astype(bf16)
            value_ref[...] = nn_dot(normed, full[:, plan.start :]).astype(bf16)


def project(plan, places, normed, grad, blocks):
    count = places.shape[0]
    rows, depth = normed.shape
    out = jax.ShapeDtypeStruct((rows, plan.wide), bf16)
    full = jax.ShapeDtypeStruct((depth, plan.both), bf16)
    return pl.pallas_call(
        functools.partial(project_kernel, plan, count, len(blocks) > count),
        out_shape=[out] * 4 + [full] * 2,
        in_specs=[SCALARS] + [WHOLE] * (2 + len(blocks)),
        out_specs=[WHOLE] * 6,
        compiler_params=room(28),
        cost_estimate=cost(8 * rows * depth * plan.wide, 4 * depth * plan.both),
        name="project",
    )(places, normed, grad, *blocks)


def label(spot, live, length):
    at = ((spot.astype(f32) + 0.5) / length.astype(f32)).astype(jnp.int32)
    return jnp.where(spot < live, at, -1)


def attend_kernel(
    plan, image_ref, query_ref, key_ref, value_ref, mixed_grad_ref,
    mixed_ref, query_grad_ref, key_grad_ref, value_grad_ref, mixed_turned, query_turned, key_sum, value_sum,
):
    rows = query_ref.shape[0]
    padded = mixed_turned.shape[1]
    scale = HEAD_DIM ** (-0.5)
    fill = jnp.zeros((padded - rows, plan.wide), bf16)
    query = jnp.concatenate([query_ref[...], fill], axis=0)
    mixed_grad = jnp.concatenate([mixed_grad_ref[...], fill], axis=0)
    key_turned = jnp.concatenate([key_ref[...], fill], axis=0).T
    value_turned = jnp.concatenate([value_ref[...], fill], axis=0).T
    live = image_ref[0] * image_ref[1]
    key_spot = lax.broadcasted_iota(jnp.int32, (rows, 1), 0)
    query_spot = lax.broadcasted_iota(jnp.int32, (1, padded), 1)
    length = jnp.full((1, 1), image_ref[1], jnp.int32)
    query_label = jnp.where(query_spot < rows, label(query_spot, live, length), -2)
    allowed = label(key_spot, live, length) == query_label
    mixed_turned[...] = jnp.zeros_like(mixed_turned)
    query_turned[...] = jnp.zeros_like(query_turned)
    key_sum[...] = jnp.zeros_like(key_sum)
    value_sum[...] = jnp.zeros_like(value_sum)
    zero = jnp.zeros((), bf16)
    for head in range(plan.heads):
        a, b, low, high = plan.window(head, 0)
        c, d, low_v, high_v = plan.window(head, plan.base)
        lane = a + lax.broadcasted_iota(jnp.int32, (1, b - a), 1)
        lane_v = c + lax.broadcasted_iota(jnp.int32, (1, d - c), 1)
        here = (lane >= low) & (lane < high)
        here_v = (lane_v >= low_v) & (lane_v < high_v)
        queries = jnp.where(here, query[:, a:b], zero)
        grads = jnp.where(here_v, mixed_grad[:, c:d], zero)
        scores = jnp.where(allowed, nt_dot(key_ref[:, a:b], queries) * scale, -1e30)
        raised = jnp.exp(scores - jnp.max(scores, axis=0, keepdims=True))
        prob = raised * (1.0 / jnp.sum(raised, axis=0, keepdims=True))
        prob_half = prob.astype(bf16)
        prob_grad = nt_dot(value_ref[:, c:d], grads)
        delta = jnp.sum(prob * prob_grad, axis=0, keepdims=True)
        score_grad = (prob * (prob_grad - delta) * scale).astype(bf16)
        row = a + lax.broadcasted_iota(jnp.int32, (b - a, 1), 0)
        row_v = c + lax.broadcasted_iota(jnp.int32, (d - c, 1), 0)
        mixed_part = nn_dot(value_turned[c:d, :rows], prob_half)
        mixed_turned[c:d, :] += jnp.where((row_v >= low_v) & (row_v < high_v), mixed_part, 0.0)
        query_part = nn_dot(key_turned[a:b, :rows], score_grad)
        query_turned[a:b, :] += jnp.where((row >= low) & (row < high), query_part, 0.0)
        value_sum[:, c:d] += nn_dot(prob_half, grads)
        key_sum[:, a:b] += nn_dot(score_grad, queries)
    mixed_ref[...] = mixed_turned[...].T[:rows].astype(bf16)
    query_grad_ref[...] = query_turned[...].T[:rows].astype(bf16)
    key_grad_ref[...] = key_sum[...].astype(bf16)
    value_grad_ref[...] = value_sum[...].astype(bf16)


def attend(plan, image, query, key, value, mixed_grad):
    rows = query.shape[0]
    padded = round_up(rows, LANES)
    out = jax.ShapeDtypeStruct((rows, plan.wide), bf16)
    return pl.pallas_call(
        functools.partial(attend_kernel, plan),
        out_shape=[out] * 4,
        in_specs=[SCALARS] + [WHOLE] * 4,
        out_specs=[WHOLE] * 4,
        scratch_shapes=[
            pltpu.VMEM((plan.wide, padded), f32),
            pltpu.VMEM((plan.wide, padded), f32),
            pltpu.VMEM((rows, plan.wide), f32),
            pltpu.VMEM((rows, plan.wide), f32),
        ],
        compiler_params=room(24),
        cost_estimate=cost(
            16 * plan.heads * rows * padded * LANES, 16 * rows * plan.wide, plan.heads * rows * padded
        ),
        name="attend",
    )(image, query, key, value, mixed_grad)


def weight_grad_kernel(plan, count, core_ref, *refs):
    spots, refs = refs[:2], refs[2:]
    normed_ref, grad_ref, mixed_ref, query_grad_ref, key_grad_ref, value_grad_ref, *outs = refs
    split, wide = plan.start, plan.wide
    depth = normed_ref.shape[1]
    pieces = 4
    step = depth // pieces
    for at in range(pieces):
        here = slice(at * step, (at + 1) * step)
        for pair, (first, second_left, second) in enumerate(
            ((query_grad_ref, grad_ref, mixed_ref), (key_grad_ref, normed_ref, value_grad_ref))
        ):
            left = tn_dot(normed_ref[:, here], first[...])
            right = tn_dot(second_left[:, here], second[...])
            seam = left[:, split:wide] + right[:, : wide - split]
            whole = jnp.concatenate([left[:, :split], seam, right[:, wide - split :]], axis=1).astype(bf16)
            if not count:
                outs[0][0, pair, here, :] = whole
                continue
            rows = depth // (2 * count)
            for two in range(count // pieces):
                chip = at * count // pieces + two
                even = whole[2 * two * rows : (2 * two + 1) * rows]
                odd = whole[(2 * two + 1) * rows : (2 * two + 2) * rows]
                first_core = core_ref[0] == 0
                outs[0][spots[0][chip], pair] = jnp.where(first_core, even, odd)
                outs[1][spots[1][chip], pair] = jnp.where(first_core, odd, even)


def weight_grads(plan, core, spots, normed, grad, mixed, query_grad, key_grad, value_grad):
    depth = normed.shape[1]
    count = spots[0].shape[0] if spots else 0
    size = (count, 2, depth // (2 * count), plan.both) if count else (1, 2, depth, plan.both)
    outs = 2 if count else 1
    if not count:
        spots = (core, core)
    return pl.pallas_call(
        functools.partial(weight_grad_kernel, plan, count),
        out_shape=[jax.ShapeDtypeStruct(size, bf16)] * outs,
        in_specs=[SCALARS] * 3 + [WHOLE] * 6,
        out_specs=[WHOLE] * outs,
        compiler_params=room(24),
        cost_estimate=cost(8 * depth * normed.shape[0] * plan.wide, 4 * depth * plan.both),
        name="weight_grads",
    )(core, *spots, normed, grad, mixed, query_grad, key_grad, value_grad)


def out_kernel(plan, *refs):
    weights, mixed, out_ref = refs[:2], refs[2:4], refs[4]
    sides, _, width = out_ref.shape
    for side in range(sides):
        here = slice(side * width, (side + 1) * width)
        out_ref[side] = sum(
            nt_dot(rows[...], weight[here, plan.start :]) for rows, weight in zip(mixed, weights)
        ).astype(bf16)


def out_parts(plan, weights, mixed, sides):
    rows = mixed[0].shape[0]
    depth = weights[0].shape[0]
    return pl.pallas_call(
        functools.partial(out_kernel, plan),
        out_shape=jax.ShapeDtypeStruct((sides, rows, depth // sides), bf16),
        in_specs=[WHOLE] * 4,
        out_specs=WHOLE,
        compiler_params=room(20),
        cost_estimate=cost(4 * rows * depth * plan.wide, 4 * depth * plan.both),
        name="out_parts",
    )(*weights, *mixed)


def norm_grad_kernel(plan, sides, side_ref, *refs):
    weights, grads, refs = refs[:4], refs[4:10], refs[10:]
    here_ref, there_ref, center_ref, inverse_ref, gain_ref, part_ref, sums_ref, held = refs
    left, right = slice(0, plan.wide), slice(plan.start, plan.both)
    width = held.shape[2]
    center, inverse = center_ref[...], inverse_ref[...]
    halves = in_order(side_ref[0], here_ref[...], there_ref[...])
    mean_a, mean_b = 0.0, 0.0
    for at in range(sides):
        here = slice(at * width, (at + 1) * width)
        grad = jnp.zeros(held.shape[1:], f32)
        for chunk in range(2):
            query, key, value = grads[3 * chunk : 3 * chunk + 3]
            qo, kv = weights[2 * chunk : 2 * chunk + 2]
            grad += nt_dot(query[...], qo[here, left])
            grad += nt_dot(key[...], kv[here, left])
            grad += nt_dot(value[...], kv[here, right])
        held[at] = grad
        product = grad * ((halves[at].astype(f32) - center) * inverse)
        sums_ref[0:1, here] = jnp.sum(product, axis=0, keepdims=True)
        sums_ref[1:2, here] = jnp.sum(grad, axis=0, keepdims=True)
        mean_a += jnp.sum(grad * gain_ref[:, here], axis=1, keepdims=True)
        mean_b += jnp.sum(product * gain_ref[:, here], axis=1, keepdims=True)
    mean_a = mean_a / (sides * width)
    mean_b = mean_b / (sides * width)
    for at in range(sides):
        scaled = held[at] * gain_ref[:, at * width : (at + 1) * width]
        normed = (halves[at].astype(f32) - center) * inverse
        part_ref[at] = (inverse * (scaled - mean_a - normed * mean_b)).astype(bf16)


def norm_grads(plan, side, weights, grads, here, there, center, inverse, gain, sides):
    rows, width = here.shape
    depth = sides * width
    return pl.pallas_call(
        functools.partial(norm_grad_kernel, plan, sides),
        out_shape=[
            jax.ShapeDtypeStruct((sides, rows, width), bf16),
            jax.ShapeDtypeStruct((2, depth), f32),
        ],
        in_specs=[SCALARS] + [WHOLE] * 15,
        out_specs=[WHOLE] * 2,
        scratch_shapes=[pltpu.VMEM((sides, rows, width), f32)],
        compiler_params=room(36),
        cost_estimate=cost(12 * rows * depth * plan.wide, 8 * depth * plan.both),
        name="norm_grads",
    )(side, *weights, *grads, here, there, center, inverse, gain)


def adam_kernel(plan, parts, scale, *refs):
    terms, refs = refs[: len(parts)], refs[len(parts) :]
    states, outs, gradient = refs[:3], refs[3:6], refs[6]
    rows = gradient.shape[0]
    here = slice(None) if rows % 16 else pl.ds(pl.multiple_of(pl.program_id(0) * rows, 16), rows)
    halves = [
        [
            sum(term[at, pair, here, :].astype(f32) for term, (half, at) in zip(terms, parts) if half == chunk)
            for pair in range(2)
        ]
        for chunk in range(2)
    ]
    for kind, (pair, side) in enumerate(((0, 0), (1, 0), (1, 1), (0, 1))):
        columns = [half[pair][:, side * plan.kind : (side + 1) * plan.kind] for half in halves]
        gradient[:, kind, :] = jnp.concatenate(columns, axis=1) * scale
    new = adam_update(*[state[here] for state in states], gradient[...], decay_rate)
    for out, value in zip(outs, new):
        out[...] = value


def adam(plan, scale, terms, states):
    shape = states[0].shape
    rows = 16 if shape[0] % 16 == 0 else shape[0]
    flat = [(term, (half, at)) for half, one in enumerate(terms) for term, at in one]
    return pl.pallas_call(
        functools.partial(adam_kernel, plan, tuple(part for _, part in flat), scale),
        grid=(shape[0] // rows,),
        out_shape=[jax.ShapeDtypeStruct(shape, f32)] * 3,
        in_specs=[WHOLE] * (len(flat) + 3),
        out_specs=[pl.BlockSpec((rows, *shape[1:]), lambda step: (step, 0, 0))] * 3,
        scratch_shapes=[pltpu.VMEM((rows, *shape[1:]), f32)],
        compiler_params=room(28),
        cost_estimate=cost(0, 6 * states[0].size * 4),
        name="adam",
    )(*[term for term, _ in flat], *states)


def ring_of(chips):
    return list(range(0, chips, 2)) + list(range(chips - 1, 0, -2))


class Ring:
    def __init__(self, devices):
        self.chips = devices // 2
        walk = ring_of(self.chips)
        self.moves, self.swap = [], [(device, device ^ 1) for device in range(devices)]
        for at, chip in enumerate(walk):
            self.moves.append((2 * chip, 2 * walk[(at + 1) % self.chips]))
            self.moves.append((2 * chip + 1, 2 * walk[(at - 1) % self.chips] + 1))
        place = {chip: at for at, chip in enumerate(walk)}
        self.arrive, self.mine, self.other = [], [], []
        for device in range(devices):
            at, core = place[device // 2], device % 2

            def come(core, step):
                return 2 * walk[(at + (step if core else -step)) % self.chips] + core

            def leave(core, step):
                return 2 * walk[(at + (1 + step if core else -1 - step)) % self.chips] + core

            steps = range(self.chips)
            self.arrive.append([come(c, s) for s in steps for c in (core, 1 - core)])
            self.mine.append([[leave(core, s) // 2 for s in steps].index(chip) for chip in steps])
            self.other.append([[leave(1 - core, s) // 2 for s in steps].index(chip) for chip in steps])

    def row(self):
        table = [a + m + o for a, m, o in zip(self.arrive, self.mine, self.other)]
        row = jnp.asarray(table, jnp.int32)[lax.axis_index("dp")]
        return jnp.split(row, [2 * self.chips, 3 * self.chips])


class Gather:
    def __init__(self, ring, block):
        self.ring, self.block, self.blocks = ring, block, []
        self.left = ring.chips - 1

    def hop(self, after):
        block = self.block = tie(self.block, after)
        if self.left:
            self.block = lax.ppermute(block, "dp", self.ring.moves)
        self.left -= 1
        self.blocks += [block, lax.ppermute(block, "dp", self.ring.swap)]
        return block


class Reduce:
    def __init__(self, ring, mine, other):
        self.ring, self.mine, self.step = ring, mine, 0
        self.near = lax.ppermute(other, "dp", ring.swap)
        self.total = self.add(0.0)
        self.left = ring.chips - 1

    def add(self, so_far):
        here = self.mine[self.step].astype(f32) + self.near[self.step].astype(f32)
        return (so_far + here).astype(bf16)

    def hop(self, after):
        sent = tie(self.total, after)
        self.come = lax.ppermute(sent, "dp", self.ring.moves)
        self.left -= 1
        self.step += 1
        self.total = self.add(self.come.astype(f32)) if self.left else self.come
        return sent

    def terms(self):
        return [(self.come[None], 0), (self.mine, self.step), (self.near, self.step)]


def tie(value, after):
    if after is None:
        return value
    return lax.optimization_barrier((value, after))[0]


def sum_over_all(values, axes):
    for axis in axes:
        size = lax.axis_size(axis)
        if size & (size - 1):
            values = lax.psum(values, axis)
            continue
        reach = 1
        while reach < size:
            swap = [(at, at ^ reach) for at in range(size)]
            values = values + lax.ppermute(values, axis, swap)
            reach *= 2
    return values


def shards(
    tokens,
    cotangent,
    master,
    moment_one,
    moment_two,
    ln_gain,
    ln_bias,
    norm_moment_one,
    norm_moment_two,
    image_count,
    tokens_per_image,
):
    groups = lax.axis_size("dp")
    sides = lax.axis_size("mp")
    side = lax.axis_index("mp")
    plan = Plan(master.shape[2])
    shard_rows = master.shape[0]
    depth = shard_rows * groups
    around = shard_rows % 16 == 0 and groups % 4 == 0
    swap_sides = [(at, at ^ 1) for at in range(sides)]
    side_now = side.astype(jnp.int32)[None]
    image = jnp.concatenate([image_count, tokens_per_image])
    gain, bias = ln_gain[None, :], ln_bias[None, :]

    packed = pack(plan, master)
    core = (lax.axis_index("dp") % 2).astype(jnp.int32)[None]
    if around:
        ring = Ring(groups)
        arrive, *spots = ring.row()
        chains = [Gather(ring, block) for block in packed]
    else:
        arrive, spots = jnp.zeros((1,), jnp.int32), ()

    last = None

    def hop(*which):
        nonlocal last
        for chain in which:
            last = chain.hop(last)

    other_tokens = lax.ppermute(tokens, "mp", swap_sides)
    other_cot = lax.ppermute(tie(cotangent, other_tokens), "mp", swap_sides)

    def norm_now():
        return norm(side_now, tie(tokens, last), other_tokens, gain, bias)

    def live_now():
        return live_rows(side_now, image, tie(cotangent, last), other_cot)

    if around:
        first_a, first_b, second = chains
        hop(first_a, first_b, second)
        hop(first_a, first_b)
        hop(first_a, first_b, second)
        hop(first_a, first_b)
        normed_low, center, inverse = norm_now()
        hop(first_a, first_b, second)
        hop(first_a, first_b)
        grad_rows = live_now()
        hop(first_a, first_b, second)
        hop(first_a, first_b)
        blocks = [first_a.blocks + first_b.blocks, second.blocks]
    else:
        normed_low, center, inverse = norm_now()
        grad_rows = live_now()
        whole = [lax.all_gather(block, "dp", axis=block.ndim - 2, tiled=True) for block in packed]
        blocks = [whole[:2], whole[2:]]

    def work(kernel, *args):
        nonlocal last
        args = list(args)
        args[0] = tie(args[0], last)
        outs = kernel(*args)
        last = outs[0]
        return outs

    def between(*which):
        if around:
            hop(*which)

    def project_now(chunk):
        query, mixed_grad, key, value, *full = work(
            lambda normed, *rest: project(plan, arrive, normed, *rest), normed_low, grad_rows, blocks[chunk]
        )
        return (query, key, value, mixed_grad), full

    def attend_now(args):
        return work(functools.partial(attend, plan, image), *args)

    def grads_now(grads):
        parts = work(
            lambda first, *rest: weight_grads(plan, core, spots, normed_low, grad_rows, first, *rest), *grads
        )
        if around:
            return Reduce(ring, *parts)
        return lax.psum_scatter(parts[0], "dp", scatter_dimension=2, tiled=True)

    def terms(total):
        return total.terms() if around else [(total, 0)]

    if around:
        hop(second)
    args, full_a = project_now(0)
    if around:
        hop(second)
    grads_a = attend_now(args)
    if around:
        hop(second)
    sum_a = grads_now(grads_a)
    if around:
        hop(second)

    between(sum_a)
    args, full_b = project_now(1)
    between(sum_a)
    grads_b = attend_now(args)
    between(sum_a)
    sum_b = grads_now(grads_b)

    between(sum_a, sum_b)
    parts = work(
        lambda first, *rest: [out_parts(plan, [full_a[0], full_b[0]], [first, *rest], sides)],
        grads_a[0],
        grads_b[0],
    )[0]
    out_away = lax.ppermute(parts[1 - side], "mp", swap_sides)
    block_out = (tokens.astype(f32) + (parts[side].astype(f32) + out_away.astype(f32))).astype(bf16)
    between(sum_a, sum_b)
    parts, sums = work(
        lambda first, *rest: norm_grads(
            plan,
            side_now,
            full_a + full_b,
            [first, *rest],
            tokens,
            other_tokens,
            center,
            inverse,
            gain,
            sides,
        ),
        *grads_a[1:],
        *grads_b[1:],
    )
    input_away = lax.ppermute(tie(parts[1 - side], out_away), "mp", swap_sides)
    live = jnp.arange(tokens.shape[0])[:, None] < image_count[0] * tokens_per_image[0]
    grad_local = jnp.where(live, cotangent, jnp.zeros((), bf16))
    input_grad = (grad_local.astype(f32) + (parts[side].astype(f32) + input_away.astype(f32))).astype(bf16)
    norm_param_grad = sum_over_all(sums, ("dp", "mp")) / groups
    new_norm, new_norm_moment_one, new_norm_moment_two = adam_update(
        jnp.stack([ln_gain, ln_bias]), norm_moment_one, norm_moment_two, norm_param_grad, 0.0
    )

    between(sum_a, sum_b)
    between(sum_a, sum_b)
    for _ in range(3):
        between(sum_b)
    new_master, new_moment_one, new_moment_two = adam(
        plan, 1.0 / groups, [terms(sum_a), terms(sum_b)], [master, moment_one, moment_two]
    )
    return (
        block_out,
        input_grad,
        new_master,
        new_moment_one,
        new_moment_two,
        new_norm[0],
        new_norm[1],
        new_norm_moment_one,
        new_norm_moment_two,
    )


def solution(mesh):
    rows = P("dp", "mp")
    cube = P("dp", None, "mp")
    return jax.shard_map(
        shards,
        mesh=mesh,
        in_specs=(rows, rows, cube, cube, cube, P(), P(), P(), P(), P("dp"), P("dp")),
        out_specs=(rows, rows, cube, cube, cube, P(), P(), P(), P()),
        check_vma=False,
    )
```

```python
import functools

import jax
import jax.numpy as jnp
from jax import lax
from jax.experimental import pallas as pl
from jax.experimental.pallas import tpu as pltpu
from jax.sharding import PartitionSpec as P

HEAD_DIM = 112
LANES = 128

eps_norm = 1e-06
beta_one = 0.9
beta_two = 0.95
learn_rate = 0.01
decay_rate = 0.1
adam_eps = 1e-08
step_count = 10.0

bf16 = jnp.bfloat16
f32 = jnp.float32
WHOLE = pl.BlockSpec(memory_space=pltpu.VMEM)
SCALARS = pl.BlockSpec(memory_space=pltpu.SMEM)
ANYWHERE = pl.BlockSpec(memory_space=pl.ANY)


def room(size):
    return pltpu.CompilerParams(vmem_limit_bytes=size * 1024 * 1024)


def cost(flops, size, exps=0):
    return pl.CostEstimate(flops=8 * flops, bytes_accessed=8 * size, transcendentals=exps)


def round_up(value, unit):
    return -(-value // unit) * unit


def nt_dot(left, right):
    return lax.dot_general(left, right, (((1,), (1,)), ((), ())), preferred_element_type=f32)


def tn_dot(left, right):
    return lax.dot_general(left, right, (((0,), (0,)), ((), ())), preferred_element_type=f32)


def nn_dot(left, right):
    return jnp.dot(left, right, preferred_element_type=f32)


def adam_update(weight_now, moment_first, moment_second, gradient, decay):
    first_new = beta_one * moment_first + (1.0 - beta_one) * gradient
    second_new = beta_two * moment_second + (1.0 - beta_two) * gradient * gradient
    first_hat = first_new / (1.0 - beta_one**step_count)
    second_hat = second_new / (1.0 - beta_two**step_count)
    weight_new = weight_now - learn_rate * (
        first_hat / (jnp.sqrt(second_hat) + adam_eps) + decay * weight_now
    )
    return (weight_new, first_new, second_new)


class Plan:
    def __init__(self, columns):
        self.kind = columns // 2
        self.both = 2 * self.kind
        self.start = self.kind // LANES * LANES
        self.base = self.kind - self.start
        self.wide = self.both - self.start
        self.heads = self.kind // HEAD_DIM

    def window(self, head, base):
        low = base + head * HEAD_DIM
        high = low + HEAD_DIM
        return (low // LANES * LANES, min(self.wide, round_up(high, LANES)), low, high)


def pack_kernel(plan, master_ref, *outs):
    for chunk, out in enumerate(outs):
        for pair, kinds in enumerate(((0, 3), (1, 2))):
            columns = [
                master_ref[:, kind, chunk * plan.kind : (chunk + 1) * plan.kind] for kind in kinds
            ]
            out[pair] = jnp.concatenate(columns, axis=1).astype(bf16)


def pack(plan, master):
    return pl.pallas_call(
        functools.partial(pack_kernel, plan),
        out_shape=[jax.ShapeDtypeStruct((2, master.shape[0], plan.both), bf16)] * 2,
        in_specs=[WHOLE],
        out_specs=[WHOLE] * 2,
        compiler_params=room(12),
        name="pack",
    )(master)


class Setup:
    def __init__(self, chips):
        self.chips = chips
        self.side, self.core, self.images, self.length = 0, 1, 2, 3
        self.arrive = 4
        self.mine = self.arrive + 2 * chips
        self.other = self.mine + chips


def in_order(side, here, there):
    return (jnp.where(side == 0, here, there), jnp.where(side == 0, there, here))


def norm_kernel(spot, setup_ref, here_ref, top_ref, low_half_ref, norm_ref, low_ref, center_ref, inverse_ref):
    there = jnp.concatenate([top_ref[...], low_half_ref[...]], axis=0)
    halves = [half.astype(f32) for half in in_order(setup_ref[spot.side], here_ref[...], there)]
    width = here_ref.shape[1]
    total = 2 * width
    center = sum(jnp.sum(half, axis=1, keepdims=True) for half in halves) / total
    shifted = [half - center for half in halves]
    spread = sum(jnp.sum(half * half, axis=1, keepdims=True) for half in shifted) / total
    inverse = lax.rsqrt(spread + eps_norm)
    center_ref[...] = center
    inverse_ref[...] = inverse
    for at, half in enumerate(shifted):
        here = slice(at * width, (at + 1) * width)
        low_ref[:, here] = (half * inverse * norm_ref[0:1, here] + norm_ref[1:2, here]).astype(bf16)


def norm(spot, setup, here, there, params):
    rows, width = here.shape
    column = jax.ShapeDtypeStruct((rows, 1), f32)
    return pl.pallas_call(
        functools.partial(norm_kernel, spot),
        out_shape=[jax.ShapeDtypeStruct((rows, 2 * width), bf16), column, column],
        in_specs=[SCALARS] + [WHOLE] * 4,
        out_specs=[WHOLE] * 3,
        compiler_params=room(10),
        cost_estimate=cost(0, 8 * rows * width),
        name="norm",
    )(setup, here, *there, params)


def live_kernel(spot, setup_ref, here_ref, top_ref, low_half_ref, out_ref):
    there = jnp.concatenate([top_ref[...], low_half_ref[...]], axis=0)
    rows, width = here_ref.shape
    row = lax.broadcasted_iota(jnp.int32, (rows, 1), 0)
    live = row < setup_ref[spot.images] * setup_ref[spot.length]
    for at, half in enumerate(in_order(setup_ref[spot.side], here_ref[...], there)):
        out_ref[:, at * width : (at + 1) * width] = jnp.where(live, half, jnp.zeros((), bf16))


def live_rows(spot, setup, here, there):
    rows, width = here.shape
    return pl.pallas_call(
        functools.partial(live_kernel, spot),
        out_shape=jax.ShapeDtypeStruct((rows, 2 * width), bf16),
        in_specs=[SCALARS] + [WHOLE] * 3,
        out_specs=WHOLE,
        compiler_params=room(8),
        cost_estimate=cost(0, 8 * rows * width),
        name="live_rows",
    )(setup, here, *there)


def project_kernel(plan, spot, count, setup_ref, normed_ref, grad_ref, *refs):
    blocks, (query_ref, mixed_grad_ref, key_ref, value_ref, *fulls) = refs[:-6], refs[-6:]
    normed = normed_ref[...]
    live = lax.broadcasted_iota(jnp.int32, (1, plan.wide), 1) >= plan.base
    for pair, full in enumerate(fulls):
        for at in range(count):
            block = blocks[at].at[pair]
            rows = block.shape[0]
            first = setup_ref[spot.arrive + at] * rows if count > 1 else 0
            if count > 1 and rows % 16 == 0:
                first = pl.multiple_of(first, 16)
            full[pl.ds(first, rows), :] = block[...]
        if pair == 0:
            query_ref[...] = nn_dot(normed, full[:, : plan.wide]).astype(bf16)
            mixed_grad = nn_dot(grad_ref[...], full[:, plan.start :])
            mixed_grad_ref[...] = jnp.where(live, mixed_grad, 0.0).astype(bf16)
        else:
            key_ref[...] = nn_dot(normed, full[:, : plan.wide]).astype(bf16)
            value_ref[...] = nn_dot(normed, full[:, plan.start :]).astype(bf16)


def project(plan, spot, count, setup, normed, grad, blocks):
    rows, depth = normed.shape
    out = jax.ShapeDtypeStruct((rows, plan.wide), bf16)
    full = jax.ShapeDtypeStruct((depth, plan.both), bf16)
    return pl.pallas_call(
        functools.partial(project_kernel, plan, spot, count),
        out_shape=[out] * 4 + [full] * 2,
        in_specs=[SCALARS] + [WHOLE] * (2 + len(blocks)),
        out_specs=[WHOLE] * 6,
        compiler_params=room(16),
        cost_estimate=cost(8 * rows * depth * plan.wide, 4 * depth * plan.both),
        name="project",
    )(setup, normed, grad, *blocks)


def label(spot, live, length):
    at = ((spot.astype(f32) + 0.5) / length.astype(f32)).astype(jnp.int32)
    return jnp.where(spot < live, at, -1)


def attend_kernel(
    plan, spot, setup_ref, query_ref, key_ref, value_ref, mixed_grad_ref,
    mixed_ref, query_grad_ref, key_grad_ref, value_grad_ref, mixed_turned, query_turned, key_sum, value_sum,
):
    rows = query_ref.shape[0]
    padded = mixed_turned.shape[1]
    scale = HEAD_DIM ** (-0.5)
    fill = jnp.zeros((padded - rows, plan.wide), bf16)
    query = jnp.concatenate([query_ref[...], fill], axis=0)
    mixed_grad = jnp.concatenate([mixed_grad_ref[...], fill], axis=0)
    key_turned = jnp.concatenate([key_ref[...], fill], axis=0).T
    value_turned = jnp.concatenate([value_ref[...], fill], axis=0).T
    live = setup_ref[spot.images] * setup_ref[spot.length]
    key_spot = lax.broadcasted_iota(jnp.int32, (rows, 1), 0)
    query_spot = lax.broadcasted_iota(jnp.int32, (1, padded), 1)
    length = jnp.full((1, 1), setup_ref[spot.length], jnp.int32)
    query_label = jnp.where(query_spot < rows, label(query_spot, live, length), -2)
    allowed = label(key_spot, live, length) == query_label
    mixed_turned[...] = jnp.zeros_like(mixed_turned)
    query_turned[...] = jnp.zeros_like(query_turned)
    key_sum[...] = jnp.zeros_like(key_sum)
    value_sum[...] = jnp.zeros_like(value_sum)
    zero = jnp.zeros((), bf16)
    for head in range(plan.heads):
        a, b, low, high = plan.window(head, 0)
        c, d, low_v, high_v = plan.window(head, plan.base)
        lane = a + lax.broadcasted_iota(jnp.int32, (1, b - a), 1)
        lane_v = c + lax.broadcasted_iota(jnp.int32, (1, d - c), 1)
        here = (lane >= low) & (lane < high)
        here_v = (lane_v >= low_v) & (lane_v < high_v)
        queries = jnp.where(here, query[:, a:b], zero)
        grads = jnp.where(here_v, mixed_grad[:, c:d], zero)
        scores = jnp.where(allowed, nt_dot(key_ref[:, a:b], queries) * scale, -1e30)
        raised = jnp.exp(scores - jnp.max(scores, axis=0, keepdims=True))
        prob = raised * (1.0 / jnp.sum(raised, axis=0, keepdims=True))
        prob_half = prob.astype(bf16)
        prob_grad = nt_dot(value_ref[:, c:d], grads)
        delta = jnp.sum(prob * prob_grad, axis=0, keepdims=True)
        score_grad = (prob * (prob_grad - delta) * scale).astype(bf16)
        row = a + lax.broadcasted_iota(jnp.int32, (b - a, 1), 0)
        row_v = c + lax.broadcasted_iota(jnp.int32, (d - c, 1), 0)
        mixed_part = nn_dot(value_turned[c:d, :rows], prob_half)
        mixed_turned[c:d, :] += jnp.where((row_v >= low_v) & (row_v < high_v), mixed_part, 0.0)
        query_part = nn_dot(key_turned[a:b, :rows], score_grad)
        query_turned[a:b, :] += jnp.where((row >= low) & (row < high), query_part, 0.0)
        value_sum[:, c:d] += nn_dot(prob_half, grads)
        key_sum[:, a:b] += nn_dot(score_grad, queries)
    mixed_ref[...] = mixed_turned[...].T[:rows].astype(bf16)
    query_grad_ref[...] = query_turned[...].T[:rows].astype(bf16)
    key_grad_ref[...] = key_sum[...].astype(bf16)
    value_grad_ref[...] = value_sum[...].astype(bf16)


def attend(plan, spot, setup, query, key, value, mixed_grad):
    rows = query.shape[0]
    padded = round_up(rows, LANES)
    out = jax.ShapeDtypeStruct((rows, plan.wide), bf16)
    return pl.pallas_call(
        functools.partial(attend_kernel, plan, spot),
        out_shape=[out] * 4,
        in_specs=[SCALARS] + [WHOLE] * 4,
        out_specs=[WHOLE] * 4,
        scratch_shapes=[
            pltpu.VMEM((plan.wide, padded), f32),
            pltpu.VMEM((plan.wide, padded), f32),
            pltpu.VMEM((rows, plan.wide), f32),
            pltpu.VMEM((rows, plan.wide), f32),
        ],
        compiler_params=room(12),
        cost_estimate=cost(
            16 * plan.heads * rows * padded * LANES, 16 * rows * plan.wide, plan.heads * rows * padded
        ),
        name="attend",
    )(setup, query, key, value, mixed_grad)


def weight_grad_kernel(plan, spot, count, setup_ref, *refs):
    normed_ref, grad_ref, mixed_ref, query_grad_ref, key_grad_ref, value_grad_ref, *outs = refs
    split, wide = plan.start, plan.wide
    depth = normed_ref.shape[1]
    pieces = 4
    step = depth // pieces
    for at in range(pieces):
        here = slice(at * step, (at + 1) * step)
        for pair, (first, second_left, second) in enumerate(
            ((query_grad_ref, grad_ref, mixed_ref), (key_grad_ref, normed_ref, value_grad_ref))
        ):
            left = tn_dot(normed_ref[:, here], first[...])
            right = tn_dot(second_left[:, here], second[...])
            seam = left[:, split:wide] + right[:, : wide - split]
            whole = jnp.concatenate([left[:, :split], seam, right[:, wide - split :]], axis=1).astype(bf16)
            if not count:
                outs[0][0, pair, here, :] = whole
                continue
            rows = depth // (2 * count)
            for two in range(count // pieces):
                chip = at * count // pieces + two
                even = whole[2 * two * rows : (2 * two + 1) * rows]
                odd = whole[(2 * two + 1) * rows : (2 * two + 2) * rows]
                first_core = setup_ref[spot.core] == 0
                outs[0][setup_ref[spot.mine + chip], pair] = jnp.where(first_core, even, odd)
                place = setup_ref[spot.other + chip]
                place = jnp.where(place == 0, count, place) - 1
                outs[2][place, pair] = jnp.where(first_core, odd, even)
    if count:
        outs[1][0] = outs[2][count - 1]


def weight_grads(plan, spot, count, setup, normed, grad, mixed, query_grad, key_grad, value_grad):
    depth = normed.shape[1]
    rows = depth // (2 * count) if count else depth
    return pl.pallas_call(
        functools.partial(weight_grad_kernel, plan, spot, count),
        out_shape=[
            jax.ShapeDtypeStruct((size, 2, rows, plan.both), bf16) for size in ((count, 1, count) if count else (1,))
        ],
        in_specs=[SCALARS] + [WHOLE] * 6,
        out_specs=[WHOLE] * (3 if count else 1),
        compiler_params=room(12),
        cost_estimate=cost(8 * depth * normed.shape[0] * plan.wide, 4 * depth * plan.both),
        name="weight_grads",
    )(setup, normed, grad, mixed, query_grad, key_grad, value_grad)


def out_kernel(plan, *refs):
    weights, mixed, out_ref = refs[:2], refs[2:4], refs[4]
    sides, _, width = out_ref.shape
    for side in range(sides):
        here = slice(side * width, (side + 1) * width)
        out_ref[side] = sum(
            nt_dot(rows[...], weight[here, plan.start :]) for rows, weight in zip(mixed, weights)
        ).astype(bf16)


def out_parts(plan, weights, mixed, sides):
    rows = mixed[0].shape[0]
    depth = weights[0].shape[0]
    return pl.pallas_call(
        functools.partial(out_kernel, plan),
        out_shape=jax.ShapeDtypeStruct((sides, rows, depth // sides), bf16),
        in_specs=[WHOLE] * 4,
        out_specs=WHOLE,
        compiler_params=room(12),
        cost_estimate=cost(4 * rows * depth * plan.wide, 4 * depth * plan.both),
        name="out_parts",
    )(*weights, *mixed)


def norm_grad_kernel(plan, spot, sides, setup_ref, *refs):
    weights, grads, refs = refs[:4], refs[4:10], refs[10:]
    here_ref, top_ref, low_half_ref, center_ref, inverse_ref, norm_ref, part_ref, sums_ref, held = refs
    left, right = slice(0, plan.wide), slice(plan.start, plan.both)
    width = held.shape[2]
    center, inverse = center_ref[...], inverse_ref[...]
    there = jnp.concatenate([top_ref[...], low_half_ref[...]], axis=0)
    halves = in_order(setup_ref[spot.side], here_ref[...], there)
    mean_a, mean_b = 0.0, 0.0
    for at in range(sides):
        here = slice(at * width, (at + 1) * width)
        grad = jnp.zeros(held.shape[1:], f32)
        for chunk in range(2):
            query, key, value = grads[3 * chunk : 3 * chunk + 3]
            qo, kv = weights[2 * chunk : 2 * chunk + 2]
            grad += nt_dot(query[...], qo[here, left])
            grad += nt_dot(key[...], kv[here, left])
            grad += nt_dot(value[...], kv[here, right])
        held[at] = grad
        product = grad * ((halves[at].astype(f32) - center) * inverse)
        sums_ref[0:1, here] = jnp.sum(product, axis=0, keepdims=True)
        sums_ref[1:2, here] = jnp.sum(grad, axis=0, keepdims=True)
        mean_a += jnp.sum(grad * norm_ref[0:1, here], axis=1, keepdims=True)
        mean_b += jnp.sum(product * norm_ref[0:1, here], axis=1, keepdims=True)
    mean_a = mean_a / (sides * width)
    mean_b = mean_b / (sides * width)
    for at in range(sides):
        scaled = held[at] * norm_ref[0:1, at * width : (at + 1) * width]
        normed = (halves[at].astype(f32) - center) * inverse
        part_ref[at] = (inverse * (scaled - mean_a - normed * mean_b)).astype(bf16)


def norm_grads(plan, spot, setup, weights, grads, here, there, center, inverse, params, sides):
    rows, width = here.shape
    depth = sides * width
    return pl.pallas_call(
        functools.partial(norm_grad_kernel, plan, spot, sides),
        out_shape=[
            jax.ShapeDtypeStruct((sides, rows, width), bf16),
            jax.ShapeDtypeStruct((2, depth), f32),
        ],
        in_specs=[SCALARS] + [WHOLE] * 16,
        out_specs=[WHOLE] * 2,
        scratch_shapes=[pltpu.VMEM((sides, rows, width), f32)],
        compiler_params=room(16),
        cost_estimate=cost(12 * rows * depth * plan.wide, 8 * depth * plan.both),
        name="norm_grads",
    )(setup, *weights, *grads, here, *there, center, inverse, params)


def adam_kernel(plan, parts, scale, *refs):
    terms, refs = refs[: len(parts)], refs[len(parts) :]
    states, outs, gradient = refs[:3], refs[3:6], refs[6]
    rows = gradient.shape[0]
    here = slice(None) if rows % 16 else pl.ds(pl.multiple_of(pl.program_id(0) * rows, 16), rows)
    halves = [
        [
            sum(term[at, pair, here, :].astype(f32) for term, (half, at) in zip(terms, parts) if half == chunk)
            for pair in range(2)
        ]
        for chunk in range(2)
    ]
    for kind, (pair, side) in enumerate(((0, 0), (1, 0), (1, 1), (0, 1))):
        columns = [half[pair][:, side * plan.kind : (side + 1) * plan.kind] for half in halves]
        gradient[:, kind, :] = jnp.concatenate(columns, axis=1) * scale
    new = adam_update(*[state[here] for state in states], gradient[...], decay_rate)
    for out, value in zip(outs, new):
        out[...] = value


def adam(plan, scale, terms, states):
    shape = states[0].shape
    rows = 16 if shape[0] % 16 == 0 else shape[0]
    flat = [(term, (half, at)) for half, one in enumerate(terms) for term, at in one]
    return pl.pallas_call(
        functools.partial(adam_kernel, plan, tuple(part for _, part in flat), scale),
        grid=(shape[0] // rows,),
        out_shape=[jax.ShapeDtypeStruct(shape, f32)] * 3,
        in_specs=[WHOLE] * (len(flat) + 3),
        out_specs=[pl.BlockSpec((rows, *shape[1:]), lambda step: (step, 0, 0))] * 3,
        scratch_shapes=[pltpu.VMEM((rows, *shape[1:]), f32)],
        compiler_params=room(16),
        cost_estimate=cost(0, 6 * states[0].size * 4),
        name="adam",
    )(*[term for term, _ in flat], *states)


def ring_of(chips):
    return list(range(0, chips, 2)) + list(range(chips - 1, 0, -2))


class Ring:
    def __init__(self, devices):
        self.chips = devices // 2
        walk = ring_of(self.chips)
        self.moves, self.swap = [], [(device, device ^ 1) for device in range(devices)]
        for at, chip in enumerate(walk):
            self.moves.append((2 * chip, 2 * walk[(at + 1) % self.chips]))
            self.moves.append((2 * chip + 1, 2 * walk[(at - 1) % self.chips] + 1))
        place = {chip: at for at, chip in enumerate(walk)}
        self.arrive, self.mine, self.other = [], [], []
        for device in range(devices):
            at, core = place[device // 2], device % 2

            def come(core, step):
                return 2 * walk[(at + (step if core else -step)) % self.chips] + core

            def leave(core, step):
                return 2 * walk[(at + (1 + step if core else -1 - step)) % self.chips] + core

            steps = range(self.chips)
            self.arrive.append([come(c, s) for s in steps for c in (core, 1 - core)])
            self.mine.append([[leave(core, s) // 2 for s in steps].index(chip) for chip in steps])
            self.other.append([[leave(1 - core, s) // 2 for s in steps].index(chip) for chip in steps])

    def table(self):
        return [a + m + o for a, m, o in zip(self.arrive, self.mine, self.other)]


class Gather:
    def __init__(self, ring, block):
        self.ring, self.block, self.blocks = ring, block, []
        self.left = ring.chips - 1

    def hop(self, after):
        block = self.block = tie(self.block, (after, self.blocks[-1:]))
        if self.left:
            self.block = lax.ppermute(block, "dp", self.ring.moves)
        self.left -= 1
        self.blocks += [block, lax.ppermute(block, "dp", self.ring.swap)]
        return block


class Reduce:
    def __init__(self, ring, mine, first, rest):
        self.ring, self.mine, self.step = ring, mine, 0
        self.first = lax.ppermute(first, "dp", ring.swap)
        self.rest = lax.ppermute(tie(rest, self.first), "dp", ring.swap)
        self.come = None

    def hop(self, after):
        if self.step == 0:
            total = self.mine[0].astype(f32) + self.first[0].astype(f32)
        else:
            total = self.total(tie(self.come, after))
        sent = tie(total.astype(bf16), after)
        self.come = lax.ppermute(sent, "dp", self.ring.moves)
        self.step += 1
        return sent

    def here(self, step):
        return self.mine[step].astype(f32) + self.rest[step - 1].astype(f32)

    def total(self, come):
        return come.astype(f32) + self.here(self.step)


def tie(value, after):
    if after is None:
        return value
    return lax.optimization_barrier((value, after))[0]


def exchanges(axis):
    size = lax.axis_size(axis)
    assert size & (size - 1) == 0
    return size.bit_length() - 1


def sums_over(values, axes):
    done = {}
    for axis in axes:
        reach = done.get(axis, 1)
        done[axis] = 2 * reach
        swap = [(at, at ^ reach) for at in range(lax.axis_size(axis))]
        there = lax.ppermute(values, axis, swap)
        after = yield values
        values = values + tie(there, after)
    yield values


def held_kernel(*refs):
    for source, target in zip(refs[:3], refs[3:]):
        target[...] = source[...]


def held(*states):
    return pl.pallas_call(
        held_kernel,
        out_shape=[jax.ShapeDtypeStruct(state.shape, f32) for state in states],
        in_specs=[WHOLE] * 3,
        out_specs=[WHOLE] * 3,
        compiler_params=room(12),
        cost_estimate=cost(0, 24 * states[0].size),
        name="held",
    )(*states)


def shards(
    tokens,
    cotangent,
    master,
    moment_one,
    moment_two,
    ln_gain,
    ln_bias,
    norm_moment_one,
    norm_moment_two,
    image_count,
    tokens_per_image,
):
    groups = lax.axis_size("dp")
    sides = lax.axis_size("mp")
    side = lax.axis_index("mp")
    plan = Plan(master.shape[2])
    shard_rows = master.shape[0]
    depth = shard_rows * groups
    around = shard_rows % 16 == 0 and groups % 8 == 0
    swap_sides = [(at, at ^ 1) for at in range(sides)]
    count = groups // 2 if around else 0
    arrivals = 2 * count if around else 1
    spot = Setup(count)
    here = lax.axis_index("dp").astype(jnp.int32)
    core, line = here % 2, here * (4 * count)
    left_side = side == 0
    side = side.astype(jnp.int32)
    master, core, line, left_side, side = lax.optimization_barrier((master, core, line, left_side, side))
    packed = pack(plan, master)

    scalars = [jnp.stack([side, core]), image_count, tokens_per_image]
    if around:
        ring = Ring(groups)
        scalars.append(lax.dynamic_slice(jnp.asarray(ring.table(), jnp.int32).reshape(-1), (line,), (4 * count,)))
        chains = [Gather(ring, block) for block in packed]
    setup = jnp.concatenate(scalars)
    live = jnp.arange(tokens.shape[0]) < image_count[0] * tokens_per_image[0]
    params = jnp.stack([ln_gain, ln_bias])

    last = None

    def hop(*which):
        nonlocal last
        for chain in which:
            last = chain.hop(last)

    def from_side(rows, before):
        cut = rows.shape[0] // 32 * 16
        parts = []
        for part in (rows[:cut], rows[cut:]):
            parts.append(lax.ppermute(tie(part, before), "mp", swap_sides))
            before = parts[-1]
        return parts

    def arrived(value):
        nonlocal last
        if around:
            last = tie(last, value)

    other_tokens = from_side(tokens, None)
    other_cot = from_side(cotangent, other_tokens[-1])

    def work(kernel, *args):
        nonlocal last
        args = list(args)
        args[0] = tie(args[0], last)
        outs = kernel(*args)
        last = outs[0]
        return outs

    def norm_now():
        return work(lambda tokens: norm(spot, setup, tokens, other_tokens, params), tokens)

    def live_now():
        return work(lambda cot: [live_rows(spot, setup, cot, other_cot)], cotangent)[0]

    if around:
        hop(*chains)
        hop(*chains)
        arrived(other_tokens[0])
        hop(*chains)
        hop(*chains)
        normed_low, center, inverse = norm_now()
        hop(*chains)
        arrived(other_cot[0])
        hop(*chains)
        hop(*chains)
        grad_rows = live_now()
        hop(*chains)
        blocks = [chain.blocks for chain in chains]
    else:
        normed_low, center, inverse = norm_now()
        grad_rows = live_now()
        blocks = [[lax.all_gather(block, "dp", axis=1, tiled=True)] for block in packed]

    def between(*which):
        if around:
            hop(*which)

    def project_now(chunk):
        query, mixed_grad, key, value, *full = work(
            lambda normed, *rest: project(plan, spot, arrivals, setup, normed, *rest),
            normed_low,
            grad_rows,
            blocks[chunk],
        )
        return (query, key, value, mixed_grad), full

    def attend_now(args):
        return work(functools.partial(attend, plan, spot, setup), *args)

    def grads_now(grads):
        parts = work(
            lambda first, *rest: weight_grads(plan, spot, count, setup, normed_low, grad_rows, first, *rest), *grads
        )
        if around:
            return Reduce(ring, *parts)
        return lax.psum_scatter(parts[0], "dp", scatter_dimension=2, tiled=True)

    def ours(parts):
        return jnp.where(left_side, parts[0], parts[1])

    def theirs(parts):
        return jnp.where(left_side, parts[1], parts[0])

    args, full_a = project_now(0)
    arrived(blocks[1])
    grads_a = attend_now(args)
    sum_a = grads_now(grads_a)

    between(sum_a)
    args, full_b = project_now(1)
    between(sum_a)
    grads_b = attend_now(args)
    sum_b = grads_now(grads_b)

    between(sum_b, sum_a)
    out_both = work(
        lambda first, *rest: [out_parts(plan, [full_a[0], full_b[0]], [first, *rest], sides)],
        grads_a[0],
        grads_b[0],
    )[0]
    out_away = lax.ppermute(theirs(out_both), "mp", swap_sides)
    between(sum_b, sum_a)
    input_both, sums = work(
        lambda first, *rest: norm_grads(
            plan,
            spot,
            setup,
            full_a + full_b,
            [first, *rest],
            tokens,
            other_tokens,
            center,
            inverse,
            params,
            sides,
        ),
        *grads_a[1:],
        *grads_b[1:],
    )
    input_away = lax.ppermute(theirs(input_both), "mp", swap_sides)
    swaps = sums_over(sums, [axis for axis in ("dp", "mp") for _ in range(exchanges(axis))])
    next(swaps)

    def swap_now():
        nonlocal last
        if around:
            last = swaps.send(last)

    between(sum_b, sum_a)
    between(sum_b, sum_a)
    swap_now()
    between(sum_b, sum_a)
    swap_now()
    block_out = work(
        lambda away: [(tokens.astype(f32) + (ours(out_both).astype(f32) + away.astype(f32))).astype(bf16)], out_away
    )[0]
    between(sum_b)
    swap_now()
    states = work(held, master, moment_one, moment_two)
    if around:
        all_a = work(lambda come: [sum_a.total(come)], sum_a.come)[0]
        rest_b = sum_b.here(ring.chips - 1)
    between(sum_b)
    swap_now()
    grad_local = jnp.where(live[:, None], cotangent, jnp.zeros((), bf16))
    input_grad = (
        grad_local.astype(f32) + (ours(input_both).astype(f32) + tie(input_away, last).astype(f32))
    ).astype(bf16)
    for all_sums in swaps:
        pass
    new_norm, new_norm_moment_one, new_norm_moment_two = adam_update(
        params, norm_moment_one, norm_moment_two, all_sums / groups, 0.0
    )
    if around:
        come, rest_b = tie((sum_b.come, rest_b), (input_grad, new_norm))
        terms = [[(all_a[None], 0)], [(come[None], 0), (rest_b[None], 0)]]
    else:
        terms = [[(sum_a, 0)], [(sum_b, 0)]]
    new_master, new_moment_one, new_moment_two = adam(plan, 1.0 / groups, terms, states)
    return (
        block_out,
        input_grad,
        new_master,
        new_moment_one,
        new_moment_two,
        new_norm[0],
        new_norm[1],
        new_norm_moment_one,
        new_norm_moment_two,
    )


def solution(mesh):
    rows = P("dp", "mp")
    cube = P("dp", None, "mp")
    return jax.shard_map(
        shards,
        mesh=mesh,
        in_specs=(rows, rows, cube, cube, cube, P(), P(), P(), P(), P("dp"), P("dp")),
        out_specs=(rows, rows, cube, cube, cube, P(), P(), P(), P()),
        check_vma=False,
    )
```

```python
import functools

import jax
import jax.numpy as jnp
from jax import lax
from jax.experimental import pallas as pl
from jax.experimental.pallas import tpu as pltpu
from jax.sharding import PartitionSpec as P

HEAD_DIM = 112
LANES = 128

eps_norm = 1e-06
beta_one = 0.9
beta_two = 0.95
learn_rate = 0.01
decay_rate = 0.1
adam_eps = 1e-08
step_count = 10.0

bf16 = jnp.bfloat16
f32 = jnp.float32
WHOLE = pl.BlockSpec(memory_space=pltpu.VMEM)
SCALARS = pl.BlockSpec(memory_space=pltpu.SMEM)
ANYWHERE = pl.BlockSpec(memory_space=pl.ANY)


def room(size):
    return pltpu.CompilerParams(vmem_limit_bytes=size * 1024 * 1024)


def cost(flops, size, exps=0):
    return pl.CostEstimate(flops=8 * flops, bytes_accessed=8 * size, transcendentals=exps)


def round_up(value, unit):
    return -(-value // unit) * unit


def nt_dot(left, right):
    return lax.dot_general(left, right, (((1,), (1,)), ((), ())), preferred_element_type=f32)


def tn_dot(left, right):
    return lax.dot_general(left, right, (((0,), (0,)), ((), ())), preferred_element_type=f32)


def nn_dot(left, right):
    return jnp.dot(left, right, preferred_element_type=f32)


def adam_update(weight_now, moment_first, moment_second, gradient, decay):
    first_new = beta_one * moment_first + (1.0 - beta_one) * gradient
    second_new = beta_two * moment_second + (1.0 - beta_two) * gradient * gradient
    first_hat = first_new / (1.0 - beta_one**step_count)
    second_hat = second_new / (1.0 - beta_two**step_count)
    weight_new = weight_now - learn_rate * (
        first_hat / (jnp.sqrt(second_hat) + adam_eps) + decay * weight_now
    )
    return (weight_new, first_new, second_new)


class Plan:
    def __init__(self, columns):
        self.kind = columns // 2
        self.both = 2 * self.kind
        self.start = self.kind // LANES * LANES
        self.base = self.kind - self.start
        self.wide = self.both - self.start
        self.heads = self.kind // HEAD_DIM

    def window(self, head, base):
        low = base + head * HEAD_DIM
        high = low + HEAD_DIM
        return (low // LANES * LANES, min(self.wide, round_up(high, LANES)), low, high)


def pack_kernel(plan, master_ref, *outs):
    for chunk, out in enumerate(outs):
        for pair, kinds in enumerate(((0, 3), (1, 2))):
            columns = [
                master_ref[:, kind, chunk * plan.kind : (chunk + 1) * plan.kind] for kind in kinds
            ]
            out[pair] = jnp.concatenate(columns, axis=1).astype(bf16)


def pack(plan, master):
    return pl.pallas_call(
        functools.partial(pack_kernel, plan),
        out_shape=[jax.ShapeDtypeStruct((2, master.shape[0], plan.both), bf16)] * 2,
        in_specs=[WHOLE],
        out_specs=[WHOLE] * 2,
        compiler_params=room(12),
        name="pack",
    )(master)


class Setup:
    def __init__(self, chips):
        self.chips = chips
        self.core, self.arrive = 0, 1
        self.mine = self.arrive + 2 * chips
        self.other = self.mine + chips


def norm_kernel(tokens_ref, norm_ref, low_ref, center_ref, inverse_ref):
    values = tokens_ref[...].astype(f32)
    center = jnp.mean(values, axis=1, keepdims=True)
    shifted = values - center
    inverse = lax.rsqrt(jnp.mean(shifted * shifted, axis=1, keepdims=True) + eps_norm)
    center_ref[...] = center
    inverse_ref[...] = inverse
    low_ref[...] = (shifted * inverse * norm_ref[0:1, :] + norm_ref[1:2, :]).astype(bf16)


def norm(tokens, params):
    rows, depth = tokens.shape
    column = jax.ShapeDtypeStruct((rows, 1), f32)
    return pl.pallas_call(
        norm_kernel,
        out_shape=[jax.ShapeDtypeStruct((rows, depth), bf16), column, column],
        in_specs=[WHOLE] * 2,
        out_specs=[WHOLE] * 3,
        compiler_params=room(12),
        cost_estimate=cost(0, 4 * rows * depth),
        name="norm",
    )(tokens, params)


def live_kernel(image_ref, length_ref, rows_ref, out_ref):
    row = lax.broadcasted_iota(jnp.int32, (rows_ref.shape[0], 1), 0)
    live = row < image_ref[0] * length_ref[0]
    out_ref[...] = jnp.where(live, rows_ref[...], jnp.zeros((), bf16))


def live_rows(images, length, rows):
    return pl.pallas_call(
        live_kernel,
        out_shape=jax.ShapeDtypeStruct(rows.shape, bf16),
        in_specs=[SCALARS, SCALARS, WHOLE],
        out_specs=WHOLE,
        compiler_params=room(8),
        cost_estimate=cost(0, 4 * rows.size),
        name="live_rows",
    )(images, length, rows)


def project_kernel(plan, spot, count, setup_ref, normed_ref, grad_ref, *refs):
    blocks, (query_ref, mixed_grad_ref, key_ref, value_ref, *fulls) = refs[:-6], refs[-6:]
    normed = normed_ref[...]
    live = lax.broadcasted_iota(jnp.int32, (1, plan.wide), 1) >= plan.base
    for pair, full in enumerate(fulls):
        for at in range(count):
            block = blocks[at].at[pair]
            rows = block.shape[0]
            first = setup_ref[spot.arrive + at] * rows if count > 1 else 0
            if count > 1 and rows % 16 == 0:
                first = pl.multiple_of(first, 16)
            full[pl.ds(first, rows), :] = block[...]
        if pair == 0:
            query_ref[...] = nn_dot(normed, full[:, : plan.wide]).astype(bf16)
            mixed_grad = nn_dot(grad_ref[...], full[:, plan.start :])
            mixed_grad_ref[...] = jnp.where(live, mixed_grad, 0.0).astype(bf16)
        else:
            key_ref[...] = nn_dot(normed, full[:, : plan.wide]).astype(bf16)
            value_ref[...] = nn_dot(normed, full[:, plan.start :]).astype(bf16)


def project(plan, spot, count, setup, normed, grad, blocks):
    rows, depth = normed.shape
    out = jax.ShapeDtypeStruct((rows, plan.wide), bf16)
    full = jax.ShapeDtypeStruct((depth, plan.both), bf16)
    return pl.pallas_call(
        functools.partial(project_kernel, plan, spot, count),
        out_shape=[out] * 4 + [full] * 2,
        in_specs=[SCALARS] + [WHOLE] * (2 + len(blocks)),
        out_specs=[WHOLE] * 6,
        compiler_params=room(16),
        cost_estimate=cost(8 * rows * depth * plan.wide, 4 * depth * plan.both),
        name="project",
    )(setup, normed, grad, *blocks)


def label(spot, live, length):
    at = ((spot.astype(f32) + 0.5) / length.astype(f32)).astype(jnp.int32)
    return jnp.where(spot < live, at, -1)


def attend_kernel(
    plan, image_ref, length_ref, query_ref, key_ref, value_ref, mixed_grad_ref,
    mixed_ref, query_grad_ref, key_grad_ref, value_grad_ref, mixed_turned, query_turned, key_sum, value_sum,
):
    rows = query_ref.shape[0]
    padded = mixed_turned.shape[1]
    scale = HEAD_DIM ** (-0.5)
    fill = jnp.zeros((padded - rows, plan.wide), bf16)
    query = jnp.concatenate([query_ref[...], fill], axis=0)
    mixed_grad = jnp.concatenate([mixed_grad_ref[...], fill], axis=0)
    key_turned = jnp.concatenate([key_ref[...], fill], axis=0).T
    value_turned = jnp.concatenate([value_ref[...], fill], axis=0).T
    live = image_ref[0] * length_ref[0]
    key_spot = lax.broadcasted_iota(jnp.int32, (rows, 1), 0)
    query_spot = lax.broadcasted_iota(jnp.int32, (1, padded), 1)
    length = jnp.full((1, 1), length_ref[0], jnp.int32)
    query_label = jnp.where(query_spot < rows, label(query_spot, live, length), -2)
    allowed = label(key_spot, live, length) == query_label
    mixed_turned[...] = jnp.zeros_like(mixed_turned)
    query_turned[...] = jnp.zeros_like(query_turned)
    key_sum[...] = jnp.zeros_like(key_sum)
    value_sum[...] = jnp.zeros_like(value_sum)
    zero = jnp.zeros((), bf16)
    for head in range(plan.heads):
        a, b, low, high = plan.window(head, 0)
        c, d, low_v, high_v = plan.window(head, plan.base)
        lane = a + lax.broadcasted_iota(jnp.int32, (1, b - a), 1)
        lane_v = c + lax.broadcasted_iota(jnp.int32, (1, d - c), 1)
        here = (lane >= low) & (lane < high)
        here_v = (lane_v >= low_v) & (lane_v < high_v)
        queries = jnp.where(here, query[:, a:b], zero)
        grads = jnp.where(here_v, mixed_grad[:, c:d], zero)
        scores = jnp.where(allowed, nt_dot(key_ref[:, a:b], queries) * scale, -1e30)
        raised = jnp.exp(scores - jnp.max(scores, axis=0, keepdims=True))
        prob = raised * (1.0 / jnp.sum(raised, axis=0, keepdims=True))
        prob_half = prob.astype(bf16)
        prob_grad = nt_dot(value_ref[:, c:d], grads)
        delta = jnp.sum(prob * prob_grad, axis=0, keepdims=True)
        score_grad = (prob * (prob_grad - delta) * scale).astype(bf16)
        row = a + lax.broadcasted_iota(jnp.int32, (b - a, 1), 0)
        row_v = c + lax.broadcasted_iota(jnp.int32, (d - c, 1), 0)
        mixed_part = nn_dot(value_turned[c:d, :rows], prob_half)
        mixed_turned[c:d, :] += jnp.where((row_v >= low_v) & (row_v < high_v), mixed_part, 0.0)
        query_part = nn_dot(key_turned[a:b, :rows], score_grad)
        query_turned[a:b, :] += jnp.where((row >= low) & (row < high), query_part, 0.0)
        value_sum[:, c:d] += nn_dot(prob_half, grads)
        key_sum[:, a:b] += nn_dot(score_grad, queries)
    mixed_ref[...] = mixed_turned[...].T[:rows].astype(bf16)
    query_grad_ref[...] = query_turned[...].T[:rows].astype(bf16)
    key_grad_ref[...] = key_sum[...].astype(bf16)
    value_grad_ref[...] = value_sum[...].astype(bf16)


def attend(plan, images, length, query, key, value, mixed_grad):
    rows = query.shape[0]
    padded = round_up(rows, LANES)
    out = jax.ShapeDtypeStruct((rows, plan.wide), bf16)
    return pl.pallas_call(
        functools.partial(attend_kernel, plan),
        out_shape=[out] * 4,
        in_specs=[SCALARS] * 2 + [WHOLE] * 4,
        out_specs=[WHOLE] * 4,
        scratch_shapes=[
            pltpu.VMEM((plan.wide, padded), f32),
            pltpu.VMEM((plan.wide, padded), f32),
            pltpu.VMEM((rows, plan.wide), f32),
            pltpu.VMEM((rows, plan.wide), f32),
        ],
        compiler_params=room(12),
        cost_estimate=cost(
            16 * plan.heads * rows * padded * LANES, 16 * rows * plan.wide, plan.heads * rows * padded
        ),
        name="attend",
    )(images, length, query, key, value, mixed_grad)


def weight_grad_kernel(plan, spot, count, setup_ref, *refs):
    normed_ref, grad_ref, mixed_ref, query_grad_ref, key_grad_ref, value_grad_ref, *outs = refs
    split, wide = plan.start, plan.wide
    depth = normed_ref.shape[1]
    pieces = 4
    step = depth // pieces
    for at in range(pieces):
        here = slice(at * step, (at + 1) * step)
        for pair, (first, second_left, second) in enumerate(
            ((query_grad_ref, grad_ref, mixed_ref), (key_grad_ref, normed_ref, value_grad_ref))
        ):
            left = tn_dot(normed_ref[:, here], first[...])
            right = tn_dot(second_left[:, here], second[...])
            seam = left[:, split:wide] + right[:, : wide - split]
            whole = jnp.concatenate([left[:, :split], seam, right[:, wide - split :]], axis=1).astype(bf16)
            if not count:
                outs[0][0, pair, here, :] = whole
                continue
            rows = depth // (2 * count)
            for two in range(count // pieces):
                chip = at * count // pieces + two
                even = whole[2 * two * rows : (2 * two + 1) * rows]
                odd = whole[(2 * two + 1) * rows : (2 * two + 2) * rows]
                first_core = setup_ref[spot.core] == 0
                outs[0][setup_ref[spot.mine + chip], pair] = jnp.where(first_core, even, odd)
                place = setup_ref[spot.other + chip]
                place = jnp.where(place == 0, count, place) - 1
                outs[2][place, pair] = jnp.where(first_core, odd, even)
    if count:
        outs[1][0] = outs[2][count - 1]


def weight_grads(plan, spot, count, setup, normed, grad, mixed, query_grad, key_grad, value_grad):
    depth = normed.shape[1]
    rows = depth // (2 * count) if count else depth
    return pl.pallas_call(
        functools.partial(weight_grad_kernel, plan, spot, count),
        out_shape=[
            jax.ShapeDtypeStruct((size, 2, rows, plan.both), bf16) for size in ((count, 1, count) if count else (1,))
        ],
        in_specs=[SCALARS] + [WHOLE] * 6,
        out_specs=[WHOLE] * (3 if count else 1),
        compiler_params=room(12),
        cost_estimate=cost(8 * depth * normed.shape[0] * plan.wide, 4 * depth * plan.both),
        name="weight_grads",
    )(setup, normed, grad, mixed, query_grad, key_grad, value_grad)


def out_kernel(plan, *refs):
    weights, mixed, out_ref = refs[:2], refs[2:4], refs[4]
    sides, _, width = out_ref.shape
    for side in range(sides):
        here = slice(side * width, (side + 1) * width)
        out_ref[side] = sum(
            nt_dot(rows[...], weight[here, plan.start :]) for rows, weight in zip(mixed, weights)
        ).astype(bf16)


def out_parts(plan, weights, mixed, sides):
    rows = mixed[0].shape[0]
    depth = weights[0].shape[0]
    return pl.pallas_call(
        functools.partial(out_kernel, plan),
        out_shape=jax.ShapeDtypeStruct((sides, rows, depth // sides), bf16),
        in_specs=[WHOLE] * 4,
        out_specs=WHOLE,
        compiler_params=room(12),
        cost_estimate=cost(4 * rows * depth * plan.wide, 4 * depth * plan.both),
        name="out_parts",
    )(*weights, *mixed)


def norm_grad_kernel(plan, sides, *refs):
    weights, grads, refs = refs[:4], refs[4:10], refs[10:]
    tokens_ref, center_ref, inverse_ref, norm_ref, part_ref, sums_ref, held = refs
    left, right = slice(0, plan.wide), slice(plan.start, plan.both)
    width = held.shape[2]
    center, inverse = center_ref[...], inverse_ref[...]
    mean_a, mean_b = 0.0, 0.0
    for at in range(sides):
        here = slice(at * width, (at + 1) * width)
        grad = jnp.zeros(held.shape[1:], f32)
        for chunk in range(2):
            query, key, value = grads[3 * chunk : 3 * chunk + 3]
            qo, kv = weights[2 * chunk : 2 * chunk + 2]
            grad += nt_dot(query[...], qo[here, left])
            grad += nt_dot(key[...], kv[here, left])
            grad += nt_dot(value[...], kv[here, right])
        held[at] = grad
        product = grad * ((tokens_ref[:, here].astype(f32) - center) * inverse)
        sums_ref[0:1, here] = jnp.sum(product, axis=0, keepdims=True)
        sums_ref[1:2, here] = jnp.sum(grad, axis=0, keepdims=True)
        mean_a += jnp.sum(grad * norm_ref[0:1, here], axis=1, keepdims=True)
        mean_b += jnp.sum(product * norm_ref[0:1, here], axis=1, keepdims=True)
    mean_a = mean_a / (sides * width)
    mean_b = mean_b / (sides * width)
    for at in range(sides):
        here = slice(at * width, (at + 1) * width)
        scaled = held[at] * norm_ref[0:1, here]
        normed = (tokens_ref[:, here].astype(f32) - center) * inverse
        part_ref[at] = (inverse * (scaled - mean_a - normed * mean_b)).astype(bf16)


def norm_grads(plan, weights, grads, tokens, center, inverse, params, sides):
    rows, depth = tokens.shape
    width = depth // sides
    return pl.pallas_call(
        functools.partial(norm_grad_kernel, plan, sides),
        out_shape=[
            jax.ShapeDtypeStruct((sides, rows, width), bf16),
            jax.ShapeDtypeStruct((2, depth), f32),
        ],
        in_specs=[WHOLE] * 14,
        out_specs=[WHOLE] * 2,
        scratch_shapes=[pltpu.VMEM((sides, rows, width), f32)],
        compiler_params=room(16),
        cost_estimate=cost(12 * rows * depth * plan.wide, 8 * depth * plan.both),
        name="norm_grads",
    )(*weights, *grads, tokens, center, inverse, params)


def adam_kernel(plan, parts, scale, *refs):
    terms, refs = refs[: len(parts)], refs[len(parts) :]
    states, outs, gradient = refs[:3], refs[3:6], refs[6]
    rows = gradient.shape[0]
    here = slice(None) if rows % 16 else pl.ds(pl.multiple_of(pl.program_id(0) * rows, 16), rows)
    halves = [
        [
            sum(term[at, pair, here, :].astype(f32) for term, (half, at) in zip(terms, parts) if half == chunk)
            for pair in range(2)
        ]
        for chunk in range(2)
    ]
    for kind, (pair, side) in enumerate(((0, 0), (1, 0), (1, 1), (0, 1))):
        columns = [half[pair][:, side * plan.kind : (side + 1) * plan.kind] for half in halves]
        gradient[:, kind, :] = jnp.concatenate(columns, axis=1) * scale
    new = adam_update(*[state[here] for state in states], gradient[...], decay_rate)
    for out, value in zip(outs, new):
        out[...] = value


def adam(plan, scale, terms, states):
    shape = states[0].shape
    rows = 16 if shape[0] % 16 == 0 else shape[0]
    flat = [(term, (half, at)) for half, one in enumerate(terms) for term, at in one]
    return pl.pallas_call(
        functools.partial(adam_kernel, plan, tuple(part for _, part in flat), scale),
        grid=(shape[0] // rows,),
        out_shape=[jax.ShapeDtypeStruct(shape, f32)] * 3,
        in_specs=[WHOLE] * (len(flat) + 3),
        out_specs=[pl.BlockSpec((rows, *shape[1:]), lambda step: (step, 0, 0))] * 3,
        scratch_shapes=[pltpu.VMEM((rows, *shape[1:]), f32)],
        compiler_params=room(16),
        cost_estimate=cost(0, 6 * states[0].size * 4),
        name="adam",
    )(*[term for term, _ in flat], *states)


def ring_of(chips):
    return list(range(0, chips, 2)) + list(range(chips - 1, 0, -2))


class Ring:
    def __init__(self, devices):
        self.chips = devices // 2
        walk = ring_of(self.chips)
        self.moves, self.swap = [], [(device, device ^ 1) for device in range(devices)]
        for at, chip in enumerate(walk):
            self.moves.append((2 * chip, 2 * walk[(at + 1) % self.chips]))
            self.moves.append((2 * chip + 1, 2 * walk[(at - 1) % self.chips] + 1))
        place = {chip: at for at, chip in enumerate(walk)}
        self.arrive, self.mine, self.other = [], [], []
        for device in range(devices):
            at, core = place[device // 2], device % 2

            def come(core, step):
                return 2 * walk[(at + (step if core else -step)) % self.chips] + core

            def leave(core, step):
                return 2 * walk[(at + (1 + step if core else -1 - step)) % self.chips] + core

            steps = range(self.chips)
            self.arrive.append([come(c, s) for s in steps for c in (core, 1 - core)])
            self.mine.append([[leave(core, s) // 2 for s in steps].index(chip) for chip in steps])
            self.other.append([[leave(1 - core, s) // 2 for s in steps].index(chip) for chip in steps])

    def table(self):
        rows = zip(self.arrive, self.mine, self.other)
        return [[device % 2] + a + m + o for device, (a, m, o) in enumerate(rows)]


class Gather:
    def __init__(self, ring, block):
        self.ring, self.block, self.blocks = ring, block, []
        self.left = ring.chips - 1

    def hop(self, after):
        block = self.block = tie(self.block, (after, self.blocks[-1:]))
        if self.left:
            self.block = lax.ppermute(block, "dp", self.ring.moves)
        self.left -= 1
        self.blocks += [block, lax.ppermute(block, "dp", self.ring.swap)]
        return block


class Reduce:
    def __init__(self, ring, mine, first, rest):
        self.ring, self.mine, self.step = ring, mine, 0
        self.first = lax.ppermute(first, "dp", ring.swap)
        self.rest = lax.ppermute(tie(rest, self.first), "dp", ring.swap)
        self.come = None

    def hop(self, after):
        if self.step == 0:
            total = self.mine[0].astype(f32) + self.first[0].astype(f32)
        else:
            total = self.total(tie(self.come, after))
        sent = tie(total.astype(bf16), after)
        self.come = lax.ppermute(sent, "dp", self.ring.moves)
        self.step += 1
        return sent

    def here(self, step, rest):
        return self.mine[step].astype(f32) + rest[step - 1].astype(f32)

    def total(self, come):
        return come.astype(f32) + self.here(self.step, self.rest)


def tie(value, after):
    if after is None:
        return value
    return lax.optimization_barrier((value, after))[0]


def exchanges(axis):
    size = lax.axis_size(axis)
    assert size & (size - 1) == 0
    return size.bit_length() - 1


def sums_over(values, axes):
    done = {}
    for axis in axes:
        reach = done.get(axis, 1)
        done[axis] = 2 * reach
        swap = [(at, at ^ reach) for at in range(lax.axis_size(axis))]
        there = lax.ppermute(values, axis, swap)
        after = yield values
        values = values + tie(there, after)
    yield values


def held_kernel(*refs):
    for source, target in zip(refs[:3], refs[3:]):
        target[...] = source[...]


def held(*states):
    return pl.pallas_call(
        held_kernel,
        out_shape=[jax.ShapeDtypeStruct(state.shape, f32) for state in states],
        in_specs=[WHOLE] * 3,
        out_specs=[WHOLE] * 3,
        compiler_params=room(12),
        cost_estimate=cost(0, 24 * states[0].size),
        name="held",
    )(*states)


def shards(
    tokens,
    cotangent,
    master,
    moment_one,
    moment_two,
    ln_gain,
    ln_bias,
    norm_moment_one,
    norm_moment_two,
    image_count,
    tokens_per_image,
):
    groups = lax.axis_size("dp")
    sides = lax.axis_size("mp")
    plan = Plan(master.shape[2])
    shard_rows = master.shape[0]
    depth = shard_rows * groups
    around = shard_rows % 16 == 0 and groups % 8 == 0
    swap_sides = [(at, at ^ 1) for at in range(sides)]
    count = groups // 2 if around else 0
    arrivals = 2 * count if around else 1
    spot = Setup(count)
    here = lax.axis_index("dp").astype(jnp.int32)
    left_side = lax.axis_index("mp") == 0
    master, here, left_side = lax.optimization_barrier((master, here, left_side))
    packed = pack(plan, master)

    if around:
        ring = Ring(groups)
        chains = [Gather(ring, block) for block in packed]
        mine = jnp.arange(groups, dtype=jnp.int32)[:, None] == here
        setup = jnp.sum(jnp.where(mine, jnp.asarray(ring.table(), jnp.int32), 0), axis=0)
    else:
        setup = jnp.zeros((1,), jnp.int32)
    live = jnp.arange(tokens.shape[0]) < image_count[0] * tokens_per_image[0]
    params = jnp.stack([ln_gain, ln_bias])

    last = None

    def hop(*which):
        nonlocal last
        for chain in which:
            last = chain.hop(last)

    def both_sides(rows, there):
        first, second = jnp.where(left_side, rows, there), jnp.where(left_side, there, rows)
        return jnp.concatenate([first, second], axis=1)

    other_tokens = lax.ppermute(tokens, "mp", swap_sides)
    other_cot = lax.ppermute(tie(cotangent, other_tokens), "mp", swap_sides)
    all_tokens = both_sides(tokens, other_tokens)
    all_cot = both_sides(cotangent, other_cot)

    def arrived(value):
        nonlocal last
        if around:
            last = (last, value)

    def work(kernel, *args):
        nonlocal last
        args = list(args)
        args[0] = tie(args[0], last)
        outs = kernel(*args)
        last = outs[0]
        return outs

    def norm_now():
        return work(lambda tokens: norm(tokens, params), all_tokens)

    def live_now():
        return work(lambda cot: [live_rows(image_count, tokens_per_image, cot)], all_cot)[0]

    if around:
        for _ in range(6):
            hop(*chains)
        normed_low, center, inverse = norm_now()
        hop(*chains)
        grad_rows = live_now()
        hop(*chains)
        blocks = [chain.blocks for chain in chains]
    else:
        normed_low, center, inverse = norm_now()
        grad_rows = live_now()
        blocks = [[lax.all_gather(block, "dp", axis=1, tiled=True)] for block in packed]

    def between(*which):
        if around:
            hop(*which)

    def project_now(chunk):
        query, mixed_grad, key, value, *full = work(
            lambda normed, *rest: project(plan, spot, arrivals, setup, normed, *rest),
            normed_low,
            grad_rows,
            blocks[chunk],
        )
        return (query, key, value, mixed_grad), full

    def attend_now(args):
        return work(functools.partial(attend, plan, image_count, tokens_per_image), *args)

    def grads_now(grads):
        parts = work(
            lambda first, *rest: weight_grads(plan, spot, count, setup, normed_low, grad_rows, first, *rest), *grads
        )
        if around:
            return Reduce(ring, *parts)
        return lax.psum_scatter(parts[0], "dp", scatter_dimension=2, tiled=True)

    def ours(parts):
        return jnp.where(left_side, parts[0], parts[1])

    def theirs(parts):
        return jnp.where(left_side, parts[1], parts[0])

    args, full_a = project_now(0)
    arrived(blocks[1])
    grads_a = attend_now(args)
    sum_a = grads_now(grads_a)

    between(sum_a)
    args, full_b = project_now(1)
    between(sum_a)
    grads_b = attend_now(args)
    sum_b = grads_now(grads_b)

    between(sum_b)
    out_both = work(
        lambda first, *rest: [out_parts(plan, [full_a[0], full_b[0]], [first, *rest], sides)],
        grads_a[0],
        grads_b[0],
    )[0]
    out_away = lax.ppermute(theirs(out_both), "mp", swap_sides)
    between(sum_a)
    between(sum_b)
    input_both, sums = work(
        lambda first, *rest: norm_grads(
            plan,
            full_a + full_b,
            [first, *rest],
            all_tokens,
            center,
            inverse,
            params,
            sides,
        ),
        *grads_a[1:],
        *grads_b[1:],
    )
    input_away = lax.ppermute(theirs(input_both), "mp", swap_sides)
    swaps = sums_over(sums, [axis for axis in ("dp", "mp") for _ in range(exchanges(axis))])
    next(swaps)

    def swap_now():
        nonlocal last
        if around:
            last = swaps.send(last)

    between(sum_b, sum_a)
    between(sum_b)
    swap_now()
    between(sum_a)
    between(sum_b)
    swap_now()
    between(sum_a)
    block_out = work(
        lambda away: [(tokens.astype(f32) + (ours(out_both).astype(f32) + away.astype(f32))).astype(bf16)], out_away
    )[0]
    between(sum_b)
    swap_now()
    between(sum_a)
    states = work(held, master, moment_one, moment_two)
    between(sum_b)
    swap_now()
    if around:
        all_a = work(lambda come: [sum_a.total(come)], sum_a.come)[0]
        rest_b = work(lambda rest: [sum_b.here(ring.chips - 1, rest)], sum_b.rest)[0]
    grad_local = jnp.where(live[:, None], cotangent, jnp.zeros((), bf16))
    input_grad = (
        grad_local.astype(f32) + (ours(input_both).astype(f32) + tie(input_away, last).astype(f32))
    ).astype(bf16)
    for all_sums in swaps:
        pass
    new_norm, new_norm_moment_one, new_norm_moment_two = adam_update(
        params, norm_moment_one, norm_moment_two, all_sums / groups, 0.0
    )
    if around:
        come, rest_b = tie((sum_b.come, rest_b), (input_grad, new_norm))
        terms = [[(all_a[None], 0)], [(come[None], 0), (rest_b[None], 0)]]
    else:
        terms = [[(sum_a, 0)], [(sum_b, 0)]]
    new_master, new_moment_one, new_moment_two = adam(plan, 1.0 / groups, terms, states)
    return (
        block_out,
        input_grad,
        new_master,
        new_moment_one,
        new_moment_two,
        new_norm[0],
        new_norm[1],
        new_norm_moment_one,
        new_norm_moment_two,
    )


def solution(mesh):
    rows = P("dp", "mp")
    cube = P("dp", None, "mp")
    return jax.shard_map(
        shards,
        mesh=mesh,
        in_specs=(rows, rows, cube, cube, cube, P(), P(), P(), P(), P("dp"), P("dp")),
        out_specs=(rows, rows, cube, cube, cube, P(), P(), P(), P()),
        check_vma=False,
    )
```

```python
import functools

import jax
import jax.numpy as jnp
from jax import lax
from jax.experimental import pallas as pl
from jax.experimental.pallas import tpu as pltpu
from jax.sharding import PartitionSpec as P

HEAD_DIM = 112
LANES = 128

eps_norm = 1e-06
beta_one = 0.9
beta_two = 0.95
learn_rate = 0.01
decay_rate = 0.1
adam_eps = 1e-08
step_count = 10.0

bf16 = jnp.bfloat16
f32 = jnp.float32
WHOLE = pl.BlockSpec(memory_space=pltpu.VMEM)
SCALARS = pl.BlockSpec(memory_space=pltpu.SMEM)
ANYWHERE = pl.BlockSpec(memory_space=pl.ANY)


def room(size):
    return pltpu.CompilerParams(vmem_limit_bytes=size * 1024 * 1024)


def cost(flops, size, exps=0):
    return pl.CostEstimate(flops=8 * flops, bytes_accessed=8 * size, transcendentals=exps)


def round_up(value, unit):
    return -(-value // unit) * unit


def nt_dot(left, right):
    return lax.dot_general(left, right, (((1,), (1,)), ((), ())), preferred_element_type=f32)


def tn_dot(left, right):
    return lax.dot_general(left, right, (((0,), (0,)), ((), ())), preferred_element_type=f32)


def nn_dot(left, right):
    return jnp.dot(left, right, preferred_element_type=f32)


def adam_update(weight_now, moment_first, moment_second, gradient, decay):
    first_new = beta_one * moment_first + (1.0 - beta_one) * gradient
    second_new = beta_two * moment_second + (1.0 - beta_two) * gradient * gradient
    first_hat = first_new / (1.0 - beta_one**step_count)
    second_hat = second_new / (1.0 - beta_two**step_count)
    weight_new = weight_now - learn_rate * (
        first_hat / (jnp.sqrt(second_hat) + adam_eps) + decay * weight_now
    )
    return (weight_new, first_new, second_new)


class Plan:
    def __init__(self, columns):
        self.kind = columns // 2
        self.both = 2 * self.kind
        self.start = self.kind // LANES * LANES
        self.base = self.kind - self.start
        self.wide = self.both - self.start
        self.heads = self.kind // HEAD_DIM

    def window(self, head, base):
        low = base + head * HEAD_DIM
        high = low + HEAD_DIM
        return (low // LANES * LANES, min(self.wide, round_up(high, LANES)), low, high)


def pack_kernel(plan, master_ref, *outs):
    for chunk, out in enumerate(outs):
        for pair, kinds in enumerate(((0, 3), (1, 2))):
            columns = [
                master_ref[:, kind, chunk * plan.kind : (chunk + 1) * plan.kind] for kind in kinds
            ]
            out[pair] = jnp.concatenate(columns, axis=1).astype(bf16)


def pack(plan, master):
    return pl.pallas_call(
        functools.partial(pack_kernel, plan),
        out_shape=[jax.ShapeDtypeStruct((2, master.shape[0], plan.both), bf16)] * 2,
        in_specs=[WHOLE],
        out_specs=[WHOLE] * 2,
        compiler_params=room(12),
        name="pack",
    )(master)


class Setup:
    def __init__(self, chips):
        self.chips = chips
        self.core, self.arrive = 0, 1
        self.mine = self.arrive + 2 * chips
        self.other = self.mine + chips


def norm_kernel(tokens_ref, norm_ref, low_ref, center_ref, inverse_ref):
    values = tokens_ref[...].astype(f32)
    center = jnp.mean(values, axis=1, keepdims=True)
    shifted = values - center
    inverse = lax.rsqrt(jnp.mean(shifted * shifted, axis=1, keepdims=True) + eps_norm)
    center_ref[...] = center
    inverse_ref[...] = inverse
    low_ref[...] = (shifted * inverse * norm_ref[0:1, :] + norm_ref[1:2, :]).astype(bf16)


def norm(tokens, params):
    rows, depth = tokens.shape
    column = jax.ShapeDtypeStruct((rows, 1), f32)
    return pl.pallas_call(
        norm_kernel,
        out_shape=[jax.ShapeDtypeStruct((rows, depth), bf16), column, column],
        in_specs=[WHOLE] * 2,
        out_specs=[WHOLE] * 3,
        compiler_params=room(12),
        cost_estimate=cost(0, 4 * rows * depth),
        name="norm",
    )(tokens, params)


def live_kernel(image_ref, length_ref, rows_ref, out_ref):
    row = lax.broadcasted_iota(jnp.int32, (rows_ref.shape[0], 1), 0)
    live = row < image_ref[0] * length_ref[0]
    out_ref[...] = jnp.where(live, rows_ref[...], jnp.zeros((), bf16))


def live_rows(images, length, rows):
    return pl.pallas_call(
        live_kernel,
        out_shape=jax.ShapeDtypeStruct(rows.shape, bf16),
        in_specs=[SCALARS, SCALARS, WHOLE],
        out_specs=WHOLE,
        compiler_params=room(8),
        cost_estimate=cost(0, 4 * rows.size),
        name="live_rows",
    )(images, length, rows)


def project_kernel(plan, spot, count, setup_ref, normed_ref, grad_ref, *refs):
    blocks, (query_ref, mixed_grad_ref, key_ref, value_ref, *fulls) = refs[:-6], refs[-6:]
    normed = normed_ref[...]
    live = lax.broadcasted_iota(jnp.int32, (1, plan.wide), 1) >= plan.base
    for pair, full in enumerate(fulls):
        for at in range(count):
            block = blocks[at].at[pair]
            rows = block.shape[0]
            first = setup_ref[spot.arrive + at] * rows if count > 1 else 0
            if count > 1 and rows % 16 == 0:
                first = pl.multiple_of(first, 16)
            full[pl.ds(first, rows), :] = block[...]
        if pair == 0:
            query_ref[...] = nn_dot(normed, full[:, : plan.wide]).astype(bf16)
            mixed_grad = nn_dot(grad_ref[...], full[:, plan.start :])
            mixed_grad_ref[...] = jnp.where(live, mixed_grad, 0.0).astype(bf16)
        else:
            key_ref[...] = nn_dot(normed, full[:, : plan.wide]).astype(bf16)
            value_ref[...] = nn_dot(normed, full[:, plan.start :]).astype(bf16)


def project(plan, spot, count, setup, normed, grad, blocks):
    rows, depth = normed.shape
    out = jax.ShapeDtypeStruct((rows, plan.wide), bf16)
    full = jax.ShapeDtypeStruct((depth, plan.both), bf16)
    return pl.pallas_call(
        functools.partial(project_kernel, plan, spot, count),
        out_shape=[out] * 4 + [full] * 2,
        in_specs=[SCALARS] + [WHOLE] * (2 + len(blocks)),
        out_specs=[WHOLE] * 6,
        compiler_params=room(16),
        cost_estimate=cost(8 * rows * depth * plan.wide, 4 * depth * plan.both),
        name="project",
    )(setup, normed, grad, *blocks)


def label(spot, live, length):
    at = ((spot.astype(f32) + 0.5) / length.astype(f32)).astype(jnp.int32)
    return jnp.where(spot < live, at, -1)


def attend_kernel(
    plan, image_ref, length_ref, query_ref, key_ref, value_ref, mixed_grad_ref,
    mixed_ref, query_grad_ref, key_grad_ref, value_grad_ref, mixed_turned, query_turned, key_sum, value_sum,
):
    rows = query_ref.shape[0]
    padded = mixed_turned.shape[1]
    scale = HEAD_DIM ** (-0.5)
    fill = jnp.zeros((padded - rows, plan.wide), bf16)
    query = jnp.concatenate([query_ref[...], fill], axis=0)
    mixed_grad = jnp.concatenate([mixed_grad_ref[...], fill], axis=0)
    key_turned = jnp.concatenate([key_ref[...], fill], axis=0).T
    value_turned = jnp.concatenate([value_ref[...], fill], axis=0).T
    live = image_ref[0] * length_ref[0]
    key_spot = lax.broadcasted_iota(jnp.int32, (rows, 1), 0)
    query_spot = lax.broadcasted_iota(jnp.int32, (1, padded), 1)
    length = jnp.full((1, 1), length_ref[0], jnp.int32)
    query_label = jnp.where(query_spot < rows, label(query_spot, live, length), -2)
    allowed = label(key_spot, live, length) == query_label
    mixed_turned[...] = jnp.zeros_like(mixed_turned)
    query_turned[...] = jnp.zeros_like(query_turned)
    key_sum[...] = jnp.zeros_like(key_sum)
    value_sum[...] = jnp.zeros_like(value_sum)
    zero = jnp.zeros((), bf16)
    for head in range(plan.heads):
        a, b, low, high = plan.window(head, 0)
        c, d, low_v, high_v = plan.window(head, plan.base)
        lane = a + lax.broadcasted_iota(jnp.int32, (1, b - a), 1)
        lane_v = c + lax.broadcasted_iota(jnp.int32, (1, d - c), 1)
        here = (lane >= low) & (lane < high)
        here_v = (lane_v >= low_v) & (lane_v < high_v)
        queries = jnp.where(here, query[:, a:b], zero)
        grads = jnp.where(here_v, mixed_grad[:, c:d], zero)
        scores = jnp.where(allowed, nt_dot(key_ref[:, a:b], queries) * scale, -1e30)
        raised = jnp.exp(scores - jnp.max(scores, axis=0, keepdims=True))
        prob = raised * (1.0 / jnp.sum(raised, axis=0, keepdims=True))
        prob_half = prob.astype(bf16)
        prob_grad = nt_dot(value_ref[:, c:d], grads)
        delta = jnp.sum(prob * prob_grad, axis=0, keepdims=True)
        score_grad = (prob * (prob_grad - delta) * scale).astype(bf16)
        row = a + lax.broadcasted_iota(jnp.int32, (b - a, 1), 0)
        row_v = c + lax.broadcasted_iota(jnp.int32, (d - c, 1), 0)
        mixed_part = nn_dot(value_turned[c:d, :rows], prob_half)
        mixed_turned[c:d, :] += jnp.where((row_v >= low_v) & (row_v < high_v), mixed_part, 0.0)
        query_part = nn_dot(key_turned[a:b, :rows], score_grad)
        query_turned[a:b, :] += jnp.where((row >= low) & (row < high), query_part, 0.0)
        value_sum[:, c:d] += nn_dot(prob_half, grads)
        key_sum[:, a:b] += nn_dot(score_grad, queries)
    mixed_ref[...] = mixed_turned[...].T[:rows].astype(bf16)
    query_grad_ref[...] = query_turned[...].T[:rows].astype(bf16)
    key_grad_ref[...] = key_sum[...].astype(bf16)
    value_grad_ref[...] = value_sum[...].astype(bf16)


def attend(plan, images, length, query, key, value, mixed_grad):
    rows = query.shape[0]
    padded = round_up(rows, LANES)
    out = jax.ShapeDtypeStruct((rows, plan.wide), bf16)
    return pl.pallas_call(
        functools.partial(attend_kernel, plan),
        out_shape=[out] * 4,
        in_specs=[SCALARS] * 2 + [WHOLE] * 4,
        out_specs=[WHOLE] * 4,
        scratch_shapes=[
            pltpu.VMEM((plan.wide, padded), f32),
            pltpu.VMEM((plan.wide, padded), f32),
            pltpu.VMEM((rows, plan.wide), f32),
            pltpu.VMEM((rows, plan.wide), f32),
        ],
        compiler_params=room(12),
        cost_estimate=cost(
            16 * plan.heads * rows * padded * LANES, 16 * rows * plan.wide, plan.heads * rows * padded
        ),
        name="attend",
    )(images, length, query, key, value, mixed_grad)


def weight_grad_kernel(plan, spot, count, setup_ref, *refs):
    normed_ref, grad_ref, mixed_ref, query_grad_ref, key_grad_ref, value_grad_ref, *outs = refs
    split, wide = plan.start, plan.wide
    depth = normed_ref.shape[1]
    pieces = 4
    step = depth // pieces
    for at in range(pieces):
        here = slice(at * step, (at + 1) * step)
        for pair, (first, second_left, second) in enumerate(
            ((query_grad_ref, grad_ref, mixed_ref), (key_grad_ref, normed_ref, value_grad_ref))
        ):
            left = tn_dot(normed_ref[:, here], first[...])
            right = tn_dot(second_left[:, here], second[...])
            seam = left[:, split:wide] + right[:, : wide - split]
            whole = jnp.concatenate([left[:, :split], seam, right[:, wide - split :]], axis=1).astype(bf16)
            if not count:
                outs[0][0, pair, here, :] = whole
                continue
            rows = depth // (2 * count)
            for two in range(count // pieces):
                chip = at * count // pieces + two
                even = whole[2 * two * rows : (2 * two + 1) * rows]
                odd = whole[(2 * two + 1) * rows : (2 * two + 2) * rows]
                first_core = setup_ref[spot.core] == 0
                outs[0][setup_ref[spot.mine + chip], pair] = jnp.where(first_core, even, odd)
                place = setup_ref[spot.other + chip]
                place = jnp.where(place == 0, count, place) - 1
                outs[2][place, pair] = jnp.where(first_core, odd, even)
    if count:
        outs[1][0] = outs[2][count - 1]


def weight_grads(plan, spot, count, setup, normed, grad, mixed, query_grad, key_grad, value_grad):
    depth = normed.shape[1]
    rows = depth // (2 * count) if count else depth
    return pl.pallas_call(
        functools.partial(weight_grad_kernel, plan, spot, count),
        out_shape=[
            jax.ShapeDtypeStruct((size, 2, rows, plan.both), bf16) for size in ((count, 1, count) if count else (1,))
        ],
        in_specs=[SCALARS] + [WHOLE] * 6,
        out_specs=[WHOLE] * (3 if count else 1),
        compiler_params=room(12),
        cost_estimate=cost(8 * depth * normed.shape[0] * plan.wide, 4 * depth * plan.both),
        name="weight_grads",
    )(setup, normed, grad, mixed, query_grad, key_grad, value_grad)


def out_kernel(plan, *refs):
    weights, mixed, out_ref = refs[:2], refs[2:4], refs[4]
    sides, _, width = out_ref.shape
    for side in range(sides):
        here = slice(side * width, (side + 1) * width)
        out_ref[side] = sum(
            nt_dot(rows[...], weight[here, plan.start :]) for rows, weight in zip(mixed, weights)
        ).astype(bf16)


def out_parts(plan, weights, mixed, sides):
    rows = mixed[0].shape[0]
    depth = weights[0].shape[0]
    return pl.pallas_call(
        functools.partial(out_kernel, plan),
        out_shape=jax.ShapeDtypeStruct((sides, rows, depth // sides), bf16),
        in_specs=[WHOLE] * 4,
        out_specs=WHOLE,
        compiler_params=room(12),
        cost_estimate=cost(4 * rows * depth * plan.wide, 4 * depth * plan.both),
        name="out_parts",
    )(*weights, *mixed)


def norm_grad_kernel(plan, side, *refs):
    weights, grads, out = refs[:4], refs[4:10], refs[10]
    left, right = slice(0, plan.wide), slice(plan.start, plan.both)
    width = out.shape[1]
    here = slice(side * width, (side + 1) * width)
    total = jnp.zeros(out.shape, f32)
    for chunk in range(2):
        query, key, value = grads[3 * chunk : 3 * chunk + 3]
        qo, kv = weights[2 * chunk : 2 * chunk + 2]
        total += nt_dot(query[...], qo[here, left])
        total += nt_dot(key[...], kv[here, left])
        total += nt_dot(value[...], kv[here, right])
    out[...] = total


def norm_grad(plan, side, sides, weights, grads):
    rows = grads[0].shape[0]
    width = weights[0].shape[0] // sides
    return pl.pallas_call(
        functools.partial(norm_grad_kernel, plan, side),
        out_shape=jax.ShapeDtypeStruct((rows, width), f32),
        in_specs=[WHOLE] * 10,
        out_specs=WHOLE,
        compiler_params=room(16),
        cost_estimate=cost(12 * rows * width * plan.wide, 8 * width * plan.both),
        name="norm_grad",
    )(*weights, *grads)


def input_grad_kernel(sides, *refs):
    grads, (tokens_ref, center_ref, inverse_ref, norm_ref, part_ref, sums_ref) = refs[:sides], refs[sides:]
    center, inverse = center_ref[...], inverse_ref[...]
    width = grads[0].shape[1]
    mean_a, mean_b = 0.0, 0.0
    for at in range(sides):
        here = slice(at * width, (at + 1) * width)
        grad = grads[at][...]
        product = grad * ((tokens_ref[:, here].astype(f32) - center) * inverse)
        sums_ref[0:1, here] = jnp.sum(product, axis=0, keepdims=True)
        sums_ref[1:2, here] = jnp.sum(grad, axis=0, keepdims=True)
        mean_a += jnp.sum(grad * norm_ref[0:1, here], axis=1, keepdims=True)
        mean_b += jnp.sum(product * norm_ref[0:1, here], axis=1, keepdims=True)
    mean_a = mean_a / (sides * width)
    mean_b = mean_b / (sides * width)
    for at in range(sides):
        here = slice(at * width, (at + 1) * width)
        scaled = grads[at][...] * norm_ref[0:1, here]
        normed = (tokens_ref[:, here].astype(f32) - center) * inverse
        part_ref[at] = (inverse * (scaled - mean_a - normed * mean_b)).astype(bf16)


def input_grads(grads, tokens, center, inverse, params):
    sides = len(grads)
    rows, depth = tokens.shape
    return pl.pallas_call(
        functools.partial(input_grad_kernel, sides),
        out_shape=[
            jax.ShapeDtypeStruct((sides, rows, depth // sides), bf16),
            jax.ShapeDtypeStruct((2, depth), f32),
        ],
        in_specs=[WHOLE] * (sides + 4),
        out_specs=[WHOLE] * 2,
        compiler_params=room(16),
        cost_estimate=cost(0, 16 * rows * depth),
        name="input_grads",
    )(*grads, tokens, center, inverse, params)


def adam_kernel(plan, parts, scale, *refs):
    terms, refs = refs[: len(parts)], refs[len(parts) :]
    states, outs, gradient = refs[:3], refs[3:6], refs[6]
    rows = gradient.shape[0]
    here = slice(None) if rows % 16 else pl.ds(pl.multiple_of(pl.program_id(0) * rows, 16), rows)
    halves = [
        [
            sum(term[at, pair, here, :].astype(f32) for term, (half, at) in zip(terms, parts) if half == chunk)
            for pair in range(2)
        ]
        for chunk in range(2)
    ]
    for kind, (pair, side) in enumerate(((0, 0), (1, 0), (1, 1), (0, 1))):
        columns = [half[pair][:, side * plan.kind : (side + 1) * plan.kind] for half in halves]
        gradient[:, kind, :] = jnp.concatenate(columns, axis=1) * scale
    new = adam_update(*[state[here] for state in states], gradient[...], decay_rate)
    for out, value in zip(outs, new):
        out[...] = value


def adam(plan, scale, terms, states):
    shape = states[0].shape
    rows = 16 if shape[0] % 16 == 0 else shape[0]
    flat = [(term, (half, at)) for half, one in enumerate(terms) for term, at in one]
    return pl.pallas_call(
        functools.partial(adam_kernel, plan, tuple(part for _, part in flat), scale),
        grid=(shape[0] // rows,),
        out_shape=[jax.ShapeDtypeStruct(shape, f32)] * 3,
        in_specs=[WHOLE] * (len(flat) + 3),
        out_specs=[pl.BlockSpec((rows, *shape[1:]), lambda step: (step, 0, 0))] * 3,
        scratch_shapes=[pltpu.VMEM((rows, *shape[1:]), f32)],
        compiler_params=room(16),
        cost_estimate=cost(0, 6 * states[0].size * 4),
        name="adam",
    )(*[term for term, _ in flat], *states)


def ring_of(chips):
    return list(range(0, chips, 2)) + list(range(chips - 1, 0, -2))


class Ring:
    def __init__(self, devices):
        self.chips = devices // 2
        walk = ring_of(self.chips)
        self.moves, self.swap = [], [(device, device ^ 1) for device in range(devices)]
        for at, chip in enumerate(walk):
            self.moves.append((2 * chip, 2 * walk[(at + 1) % self.chips]))
            self.moves.append((2 * chip + 1, 2 * walk[(at - 1) % self.chips] + 1))
        place = {chip: at for at, chip in enumerate(walk)}
        self.arrive, self.mine, self.other = [], [], []
        for device in range(devices):
            at, core = place[device // 2], device % 2

            def come(core, step):
                return 2 * walk[(at + (step if core else -step)) % self.chips] + core

            def leave(core, step):
                return 2 * walk[(at + (1 + step if core else -1 - step)) % self.chips] + core

            steps = range(self.chips)
            self.arrive.append([come(c, s) for s in steps for c in (core, 1 - core)])
            self.mine.append([[leave(core, s) // 2 for s in steps].index(chip) for chip in steps])
            self.other.append([[leave(1 - core, s) // 2 for s in steps].index(chip) for chip in steps])

    def table(self):
        rows = zip(self.arrive, self.mine, self.other)
        return [[device % 2] + a + m + o for device, (a, m, o) in enumerate(rows)]


class Gather:
    def __init__(self, ring, block):
        self.ring, self.block, self.blocks = ring, block, []
        self.left = ring.chips - 1

    def hop(self, after):
        block = self.block = tie(self.block, (after, self.blocks[-1:]))
        if self.left:
            self.block = lax.ppermute(block, "dp", self.ring.moves)
        self.left -= 1
        self.blocks += [block, lax.ppermute(block, "dp", self.ring.swap)]
        return block


class Reduce:
    def __init__(self, ring, mine, first, rest):
        self.ring, self.mine, self.step = ring, mine, 0
        self.first = lax.ppermute(first, "dp", ring.swap)
        self.rest = lax.ppermute(tie(rest, self.first), "dp", ring.swap)
        self.come = None

    def hop(self, after):
        if self.step == 0:
            total = self.mine[0].astype(f32) + self.first[0].astype(f32)
        else:
            total = self.total(tie(self.come, after))
        sent = tie(total.astype(bf16), after)
        self.come = lax.ppermute(sent, "dp", self.ring.moves)
        self.step += 1
        return sent

    def here(self, step, rest):
        return self.mine[step].astype(f32) + rest[step - 1].astype(f32)

    def total(self, come):
        return come.astype(f32) + self.here(self.step, self.rest)


def tie(value, after):
    if after is None:
        return value
    return lax.optimization_barrier((value, after))[0]


def exchanges(axis):
    size = lax.axis_size(axis)
    assert size & (size - 1) == 0
    return size.bit_length() - 1


def sums_over(values, axes):
    done = {}
    for axis in axes:
        reach = done.get(axis, 1)
        done[axis] = 2 * reach
        swap = [(at, at ^ reach) for at in range(lax.axis_size(axis))]
        there = lax.ppermute(values, axis, swap)
        after = yield values
        values = values + tie(there, after)
    yield values


def held_kernel(*refs):
    for source, target in zip(refs[:3], refs[3:]):
        target[...] = source[...]


def held(*states):
    return pl.pallas_call(
        held_kernel,
        out_shape=[jax.ShapeDtypeStruct(state.shape, f32) for state in states],
        in_specs=[WHOLE] * 3,
        out_specs=[WHOLE] * 3,
        compiler_params=room(12),
        cost_estimate=cost(0, 24 * states[0].size),
        name="held",
    )(*states)


def shards(
    tokens,
    cotangent,
    master,
    moment_one,
    moment_two,
    ln_gain,
    ln_bias,
    norm_moment_one,
    norm_moment_two,
    image_count,
    tokens_per_image,
):
    groups = lax.axis_size("dp")
    sides = lax.axis_size("mp")
    plan = Plan(master.shape[2])
    shard_rows = master.shape[0]
    depth = shard_rows * groups
    around = shard_rows % 16 == 0 and groups % 8 == 0
    swap_sides = [(at, at ^ 1) for at in range(sides)]
    count = groups // 2 if around else 0
    arrivals = 2 * count if around else 1
    spot = Setup(count)
    here = lax.axis_index("dp").astype(jnp.int32)
    left_side = lax.axis_index("mp") == 0
    master, here, left_side = lax.optimization_barrier((master, here, left_side))
    packed = pack(plan, master)

    if around:
        ring = Ring(groups)
        chains = [Gather(ring, block) for block in packed]
        mine = jnp.arange(groups, dtype=jnp.int32)[:, None] == here
        setup = jnp.sum(jnp.where(mine, jnp.asarray(ring.table(), jnp.int32), 0), axis=0)
    else:
        setup = jnp.zeros((1,), jnp.int32)
    live = jnp.arange(tokens.shape[0]) < image_count[0] * tokens_per_image[0]
    params = jnp.stack([ln_gain, ln_bias])

    last = None

    def hop(*which):
        nonlocal last
        for chain in which:
            last = chain.hop(last)

    def both_sides(rows, there):
        first, second = jnp.where(left_side, rows, there), jnp.where(left_side, there, rows)
        return jnp.concatenate([first, second], axis=1)

    other_tokens = lax.ppermute(tokens, "mp", swap_sides)
    other_cot = lax.ppermute(tie(cotangent, other_tokens), "mp", swap_sides)
    all_tokens = both_sides(tokens, other_tokens)
    all_cot = both_sides(cotangent, other_cot)

    def arrived(value):
        nonlocal last
        if around:
            last = (last, value)

    def work(kernel, *args):
        nonlocal last
        args = list(args)
        args[0] = tie(args[0], last)
        outs = kernel(*args)
        last = outs[0]
        return outs

    def norm_now():
        return work(lambda tokens: norm(tokens, params), all_tokens)

    def live_now():
        return work(lambda cot: [live_rows(image_count, tokens_per_image, cot)], all_cot)[0]

    if around:
        for _ in range(6):
            hop(*chains)
        normed_low, center, inverse = norm_now()
        hop(*chains)
        grad_rows = live_now()
        hop(*chains)
        blocks = [chain.blocks for chain in chains]
    else:
        normed_low, center, inverse = norm_now()
        grad_rows = live_now()
        blocks = [[lax.all_gather(block, "dp", axis=1, tiled=True)] for block in packed]

    def between(*which):
        if around:
            hop(*which)

    def project_now(chunk):
        query, mixed_grad, key, value, *full = work(
            lambda normed, *rest: project(plan, spot, arrivals, setup, normed, *rest),
            normed_low,
            grad_rows,
            blocks[chunk],
        )
        return (query, key, value, mixed_grad), full

    def attend_now(args):
        return work(functools.partial(attend, plan, image_count, tokens_per_image), *args)

    def grads_now(grads):
        parts = work(
            lambda first, *rest: weight_grads(plan, spot, count, setup, normed_low, grad_rows, first, *rest), *grads
        )
        if around:
            return Reduce(ring, *parts)
        return lax.psum_scatter(parts[0], "dp", scatter_dimension=2, tiled=True)

    def ours(parts):
        return jnp.where(left_side, parts[0], parts[1])

    def theirs(parts):
        return jnp.where(left_side, parts[1], parts[0])

    args, full_a = project_now(0)
    arrived(blocks[1])
    grads_a = attend_now(args)
    sum_a = grads_now(grads_a)

    args, full_b = project_now(1)
    between(sum_a)
    grads_b = attend_now(args)
    sum_b = grads_now(grads_b)

    between(sum_b)
    out_both = work(
        lambda first, *rest: [out_parts(plan, [full_a[0], full_b[0]], [first, *rest], sides)],
        grads_a[0],
        grads_b[0],
    )[0]
    out_away = lax.ppermute(theirs(out_both), "mp", swap_sides)
    halves = []
    for at in range(sides):
        halves += work(
            lambda first, *rest: [norm_grad(plan, at, sides, full_a + full_b, [first, *rest])],
            *grads_a[1:],
            *grads_b[1:],
        )
        between((sum_a, sum_b)[at % 2])
    input_both, sums = work(
        lambda first, *rest: input_grads([first, *rest], all_tokens, center, inverse, params), *halves
    )
    input_away = lax.ppermute(theirs(input_both), "mp", swap_sides)
    swaps = sums_over(sums, [axis for axis in ("dp", "mp") for _ in range(exchanges(axis))])
    next(swaps)

    def swap_now():
        nonlocal last
        if around:
            last = swaps.send(last)

    between(sum_a)
    swap_now()
    between(sum_b)
    between(sum_a)
    swap_now()
    between(sum_b)
    block_out = work(
        lambda away: [(tokens.astype(f32) + (ours(out_both).astype(f32) + away.astype(f32))).astype(bf16)], out_away
    )[0]
    between(sum_a)
    swap_now()
    between(sum_b)
    between(sum_a)
    swap_now()
    between(sum_b)
    grad_local = jnp.where(live[:, None], cotangent, jnp.zeros((), bf16))
    input_grad = work(
        lambda away: [(grad_local.astype(f32) + (ours(input_both).astype(f32) + away.astype(f32))).astype(bf16)],
        input_away,
    )[0]
    between(sum_a)
    states = work(held, master, moment_one, moment_two)
    between(sum_b)
    if around:
        assert sum_a.step == sum_b.step == ring.chips - 1
        all_sums = swaps.send(last)
        all_a = work(lambda come: [sum_a.total(come)], sum_a.come)[0]
        rest_b = work(lambda rest: [sum_b.here(ring.chips - 1, rest)], sum_b.rest)[0]
    else:
        for all_sums in swaps:
            pass
    new_norm, new_norm_moment_one, new_norm_moment_two = adam_update(
        params, norm_moment_one, norm_moment_two, all_sums / groups, 0.0
    )
    if around:
        come, rest_b = tie((sum_b.come, rest_b), new_norm)
        terms = [[(all_a[None], 0)], [(come[None], 0), (rest_b[None], 0)]]
    else:
        terms = [[(sum_a, 0)], [(sum_b, 0)]]
    new_master, new_moment_one, new_moment_two = adam(plan, 1.0 / groups, terms, states)
    return (
        block_out,
        input_grad,
        new_master,
        new_moment_one,
        new_moment_two,
        new_norm[0],
        new_norm[1],
        new_norm_moment_one,
        new_norm_moment_two,
    )


def solution(mesh):
    rows = P("dp", "mp")
    cube = P("dp", None, "mp")
    return jax.shard_map(
        shards,
        mesh=mesh,
        in_specs=(rows, rows, cube, cube, cube, P(), P(), P(), P(), P("dp"), P("dp")),
        out_specs=(rows, rows, cube, cube, cube, P(), P(), P(), P()),
        check_vma=False,
    )
```
